32 devices in a mesh: grp: 16 (over z, x, core), swap: 2 (over y).
Axes of the slice: x: 2, y: 2, z: 4, core: 2. Of those that a mesh axis runs over, the one named last changes fastest.
Arguments:
- samples: bfloat16 [2, 16, 64, 4, 4096], P('swap', 'grp'), may hold values from 0.049804688 to 4
- tile_list: int32 [2, 16, 64], replicated, may hold values from 0 to 127, as said below
- tile_slot: int32 [128], replicated, may hold values from 0 to 127, as said below
- brick_rank: int32 [2, 128], replicated, may hold values from 0 to 127, each once within a row
Outputs:
- final_image: float32 [16, 8, 4, 4096], P('grp', None, None, 'swap')
The draws below stay inside these ranges and needn't reach their ends.
Inputs may be any that keep to these rules, and one draw needn't show every extreme that they name: `tile_list`: the 64 tiles of one device are distinct; fragments b * 8 to (b + 1) * 8 - 1 of a device belong to its brick b. With owner(t) = tile_slot[t] // 8, each device has 8 tiles of each of a quarter of the owners of its group, 4 of each of half of them and none of the rest; in every slab one owner has 8 tiles from every device of the group. A permutation: tile t is row tile_slot[t] % 8 of owner tile_slot[t] // 8.
All inputs are finite; a program needn't handle non-finite values.
Results may differ from the reference program's by a relative error of at most 0.0003.
Values sent between devices are 32-bit elements; how exact they have to be, the bound alone decides.
No kernel may reach another device: no remote copies, remote signals or barrier semaphores. Data moves between devices by JAX's collectives and lax.ppermute only.
A program may use at most 64 MiB of HBM per device.

```python
import math
import jax
import jax.numpy as jnp
from jax import lax

TILE_PIX = 4096
DEPTH = 4
BRICKS = 8
OWN = 8
FOOT = 64
CAP = 8
SCREEN = 128
N_GRP = 16
N_SWAP = 2


def layout(key):
    base_key = jax.random.fold_in(key, 7)
    tile_slot = jax.random.permutation(jax.random.fold_in(base_key, 1), SCREEN).astype(jnp.int32)
    slot_tile = jnp.argsort(tile_slot).astype(jnp.int32)
    hot_owner = jax.random.randint(jax.random.fold_in(base_key, 2), (N_SWAP,), 0, N_GRP)
    position = jnp.arange(N_GRP, dtype=jnp.int32)
    pattern = jnp.where(position < N_GRP // 4, CAP, jnp.where(position < 3 * N_GRP // 4, CAP // 2, 0))
    scores = jax.random.randint(jax.random.fold_in(base_key, 3), (N_SWAP, N_GRP, N_GRP), 0, 2 ** 20) * N_GRP + position
    scores = jnp.where(position[None, None, :] == hot_owner[:, None, None], -1, scores)
    owner_order = jnp.argsort(scores, axis=-1).astype(jnp.int32)
    within = jnp.arange(OWN, dtype=jnp.int32)
    picked_score = jax.random.randint(jax.random.fold_in(base_key, 4), (N_SWAP, N_GRP, N_GRP, OWN), 0, 2 ** 20) * OWN + within
    picked = jnp.argsort(picked_score, axis=-1)[..., :CAP].astype(jnp.int32)
    chosen = slot_tile[owner_order[..., None] * OWN + picked]
    live_slot = jnp.arange(CAP, dtype=jnp.int32)[None, None, None, :] < pattern[None, None, :, None]
    live_slot = jnp.broadcast_to(live_slot, (N_SWAP, N_GRP, N_GRP, CAP)).reshape(N_SWAP, N_GRP, N_GRP * CAP)
    flat_tiles = chosen.reshape(N_SWAP, N_GRP, N_GRP * CAP)
    rank_key = jnp.where(live_slot, 0, 1) * (N_GRP * CAP) + jnp.arange(N_GRP * CAP, dtype=jnp.int32)
    kept_order = jnp.argsort(rank_key, axis=-1)[..., :FOOT]
    tile_ids = jnp.take_along_axis(flat_tiles, kept_order, axis=-1)
    shuffle_score = jax.random.randint(jax.random.fold_in(base_key, 5), (N_SWAP, N_GRP, FOOT), 0, 2 ** 20) * FOOT + jnp.arange(FOOT, dtype=jnp.int32)
    shuffled = jnp.argsort(shuffle_score, axis=-1)
    tile_ids = jnp.take_along_axis(tile_ids, shuffled, axis=-1)
    return (tile_ids.astype(jnp.int32), tile_slot)


def draw_tile_list(key, part):
    return layout(key)[0]


def draw_tile_slot(key, part):
    return layout(key)[1]


def shard_levels(stream_key, extent, shards, least, top_value):
    gain = 1.0
    for axis_at, parts in shards:
        steps = jax.random.uniform(jax.random.fold_in(jax.random.fold_in(stream_key, 6), axis_at), (parts,), jnp.float32, least / len(shards), top_value / len(shards))
        gain = gain * jnp.repeat(jnp.exp(steps), extent[axis_at] // parts).reshape((-1,) + (1,) * (len(extent) - 1 - axis_at))
    return gain


def setup_inputs(seed: int = 0) -> dict:
    splits = jax.random.split(jax.random.key(seed), 5)
    samples = jnp.clip(jnp.exp(math.log(4.0) - 4.3859405 * jax.random.uniform(splits[0], (N_SWAP, N_GRP, FOOT, DEPTH, TILE_PIX), jnp.float32) ** shard_levels(splits[0], (N_SWAP, N_GRP, FOOT, DEPTH, TILE_PIX), ((0, 2), (1, 16)), -0.2, 0.2)), 0.049804688, 4.0).astype(jnp.bfloat16)
    tile_list = draw_tile_list(jax.random.fold_in(splits[4], 71), 0)
    tile_slot = draw_tile_slot(jax.random.fold_in(splits[4], 71), 0)
    brick_rank = jax.vmap(lambda own: jax.random.permutation(own, N_GRP * BRICKS))(jax.random.split(splits[3], N_SWAP)).reshape((N_SWAP, N_GRP * BRICKS)).astype(jnp.int32)
    return dict(samples=samples, tile_list=tile_list, tile_slot=tile_slot, brick_rank=brick_rank)


EXTINCTION = 0.024


def render(values_in):
    depth_count = values_in.shape[1]
    shape = (values_in.shape[0], values_in.shape[2])
    before = jnp.zeros(shape, jnp.float32)
    red_sum = jnp.zeros(shape, jnp.float32)
    green_sum = jnp.zeros(shape, jnp.float32)
    blue_sum = jnp.zeros(shape, jnp.float32)
    for level in range(depth_count):
        values = values_in[:, level].astype(jnp.float32)
        extinction = EXTINCTION * values
        weight = jnp.exp(-before) * (1.0 - jnp.exp(-extinction))
        ratio = values / (1.0 + values)
        red_sum = red_sum + weight * ratio
        green_sum = green_sum + weight * 4.0 * ratio * (1.0 - ratio)
        blue_sum = blue_sum + weight * (1.0 - ratio)
        before = before + extinction
    return jnp.stack([red_sum, green_sum, blue_sum, before], axis=1)


def reference(samples, tile_list, tile_slot, brick_rank):
    swap_count, group_count, per_device = tile_list.shape
    per_brick = per_device // BRICKS
    flattened = samples.reshape(swap_count * group_count * per_device, DEPTH, TILE_PIX)
    tile_ids = tile_list.reshape(-1).astype(jnp.int32)
    brick_ranks = jnp.repeat(brick_rank.reshape(swap_count, group_count, BRICKS), per_brick, axis=2)
    slab_ids = jnp.arange(swap_count, dtype=jnp.int32)[:, None, None]
    frag_keys = (slab_ids * (group_count * BRICKS) + brick_ranks).reshape(-1).astype(jnp.int32)
    visit_order = jnp.argsort(frag_keys).astype(jnp.int32)
    screen_tiles = tile_slot.shape[0]

    def advance(carry, frag_index):
        colors, optical = carry
        fragment = render(lax.dynamic_slice_in_dim(flattened, frag_index, 1, 0))[0]
        tile_id = tile_ids[frag_index]
        seen_depth = lax.dynamic_index_in_dim(optical, tile_id, 0, keepdims=False)
        old_color = lax.dynamic_index_in_dim(colors, tile_id, 0, keepdims=False)
        colors = lax.dynamic_update_index_in_dim(colors, old_color + jnp.exp(-seen_depth)[None] * fragment[:3], tile_id, 0)
        optical = lax.dynamic_update_index_in_dim(optical, seen_depth + fragment[3], tile_id, 0)
        return (colors, optical), None

    initial = (jnp.zeros((screen_tiles, 3, TILE_PIX), jnp.float32), jnp.zeros((screen_tiles, TILE_PIX), jnp.float32))
    (colors, optical), _ = lax.scan(advance, initial, visit_order)
    slot_tile = jnp.argsort(tile_slot).astype(jnp.int32)
    colors = colors[slot_tile]
    optical = optical[slot_tile]
    final_image = jnp.concatenate([colors, (1.0 - jnp.exp(-optical))[:, None]], axis=1)
    return final_image.reshape(N_GRP, OWN, 4, TILE_PIX)
```

```python
import functools
import jax
import jax.numpy as jnp
from jax import lax
from jax.experimental import pallas as pl
from jax.experimental.pallas import tpu as pltpu
from jax.sharding import PartitionSpec as P

BRICKS = 8


EXTINCTION = 0.024


def from_partner(array, axis, apart):
    return lax.ppermute(array, axis, [(i, i ^ 1 << apart) for i in range(lax.axis_size(axis))])


def render(values_in):
    depth_count = values_in.shape[1]
    shape = (values_in.shape[0], values_in.shape[2])
    before = jnp.zeros(shape, jnp.float32)
    red_sum = jnp.zeros(shape, jnp.float32)
    green_sum = jnp.zeros(shape, jnp.float32)
    blue_sum = jnp.zeros(shape, jnp.float32)
    for level in range(depth_count):
        values = values_in[:, level].astype(jnp.float32)
        extinction = EXTINCTION * values
        weight = jnp.exp(-before) * (1.0 - jnp.exp(-extinction))
        ratio = values / (1.0 + values)
        red_sum = red_sum + weight * ratio
        green_sum = green_sum + weight * 4.0 * ratio * (1.0 - ratio)
        blue_sum = blue_sum + weight * (1.0 - ratio)
        before = before + extinction
    return jnp.stack([red_sum, green_sum, blue_sum, before], axis=1)


def over_pair(front_part, back_part):
    colors = front_part[:, :3] + jnp.exp(-front_part[:, 3:4]) * back_part[:, :3]
    return jnp.concatenate([colors, front_part[:, 3:4] + back_part[:, 3:4]], axis=1)


def slot_tables(tiles_in, tile_slot, owned, per_brick, ranks_in):
    group_count, per_device = tiles_in.shape
    slot_ids = tile_slot[tiles_in]
    owners = slot_ids // owned
    tile_rows = slot_ids % owned
    position = jnp.arange(per_device, dtype=jnp.int32)
    same_owner = (owners[:, :, None] == owners[:, None, :]) & (
        position[None, None, :] < position[None, :, None]
    )
    places = jnp.sum(same_owner.astype(jnp.int32), axis=2)
    depth_keys = jnp.repeat(ranks_in.reshape(group_count, BRICKS), per_brick, axis=1)
    return (owners, tile_rows, places, depth_keys)


def arrivals(owners, tile_rows, places, depth_keys, device, capacity):
    slot_ids = jnp.arange(capacity, dtype=jnp.int32)
    matched = (
        (owners[:, None, :] == device) & (places[:, None, :] == slot_ids[None, :, None])
    ).astype(jnp.int32)
    rows_in = jnp.sum(matched * tile_rows[:, None, :], axis=2).reshape(-1)
    keys_in = jnp.sum(matched * depth_keys[:, None, :], axis=2).reshape(-1)
    valid_in = (jnp.sum(matched, axis=2) > 0).reshape(-1)
    return (rows_in, keys_in, valid_in)


def outgoing(fragments, owners_mine, places_mine, group_count, capacity):
    per_device = fragments.shape[0]
    target = owners_mine * capacity + places_mine
    slot_ids = jnp.arange(group_count * capacity, dtype=jnp.int32)
    matched = (target[None, :] == slot_ids[:, None]).astype(jnp.int32)
    numbers = jnp.arange(per_device, dtype=jnp.int32) + 1
    source = jnp.sum(matched * numbers[None, :], axis=1) - 1
    source = jnp.where(source < 0, per_device, source)
    padded = jnp.concatenate(
        [fragments, jnp.zeros((1,) + fragments.shape[1:], jnp.float32)], axis=0
    )
    return jnp.take(padded, source, axis=0)


def combine(pieces, rows_in, keys_in, valid_in, owned):
    optical = pieces[:, 3]
    both_valid = valid_in[:, None] & valid_in[None, :]
    in_front = (
        (rows_in[:, None] == rows_in[None, :]) & both_valid & (keys_in[None, :] < keys_in[:, None])
    ).astype(jnp.float32)
    prefix = jnp.dot(
        in_front, optical, precision=lax.Precision.HIGHEST, preferred_element_type=jnp.float32
    )
    shaded = pieces[:, :3] * jnp.exp(-prefix)[:, None]
    to_rows = (
        (jnp.arange(owned, dtype=jnp.int32)[:, None] == rows_in[None, :]) & valid_in[None, :]
    ).astype(jnp.float32)
    colors = jnp.einsum("of,fcp->ocp", to_rows, shaded, precision=lax.Precision.HIGHEST)
    summed = jnp.dot(
        to_rows, optical, precision=lax.Precision.HIGHEST, preferred_element_type=jnp.float32
    )
    return jnp.concatenate([colors, summed[:, None]], axis=1)


def leaving_of(fragments, owners_slab, places_slab, device, group_count, capacity):
    owners_mine = lax.dynamic_index_in_dim(owners_slab, device, 0, keepdims=False)
    places_mine = lax.dynamic_index_in_dim(places_slab, device, 0, keepdims=False)
    return outgoing(fragments, owners_mine, places_mine, group_count, capacity)


def general_shards(samples, tile_list, tile_slot, brick_rank):
    group_count = lax.axis_size("grp")
    swap_count = lax.axis_size("swap")
    device = lax.axis_index("grp")
    slab = lax.axis_index("swap")
    per_device = tile_list.shape[2]
    per_brick = per_device // BRICKS
    owned = tile_slot.shape[0] // group_count
    capacity = 2 * per_device // group_count
    pixels = samples.shape[4]
    block = pixels // swap_count
    fragments = render(samples[0, 0])
    tiles_slab = lax.dynamic_index_in_dim(tile_list, slab, 0, keepdims=False)
    ranks_slab = lax.dynamic_index_in_dim(brick_rank, slab, 0, keepdims=False)
    owners_slab, rows_slab, places_slab, keys_slab = slot_tables(
        tiles_slab, tile_slot, owned, per_brick, ranks_slab
    )
    leaving = leaving_of(fragments, owners_slab, places_slab, device, group_count, capacity)
    rows_in, keys_in, valid_in = arrivals(
        owners_slab, rows_slab, places_slab, keys_slab, device, capacity
    )
    arrived = lax.all_to_all(
        leaving.reshape(group_count, capacity, 4, pixels),
        "grp",
        split_axis=0,
        concat_axis=0,
        tiled=True,
    )
    partial_value = combine(
        arrived.reshape(-1, 4, arrived.shape[3]), rows_in, keys_in, valid_in, owned
    )
    levels = swap_count.bit_length() - 1
    partial_value = partial_value.reshape((owned, 4) + (2,) * levels + (block,))
    for level in range(levels):
        lower = partial_value[..., 0, :]
        upper = partial_value[..., 1, :]
        my_bit = jnp.right_shift(slab, level) % 2
        kept = jnp.where(my_bit == 1, upper, lower)
        given = jnp.where(my_bit == 1, lower, upper)
        received = from_partner(given, "swap", level)
        front_part = jnp.where(my_bit == 0, kept, received)
        back_part = jnp.where(my_bit == 0, received, kept)
        partial_value = over_pair(front_part, back_part)
    final_image = jnp.concatenate(
        [partial_value[:, :3], 1.0 - jnp.exp(-partial_value[:, 3:4])], axis=1
    )
    return final_image[None]


LANES = 128
VMEM_BYTES = 48 * 1024 * 1024


def render_kernel(samples_ref, out_ref):
    depth_count = samples_ref.shape[0]
    for part in range(out_ref.shape[0]):
        lanes = slice(part * LANES, (part + 1) * LANES)
        before = None
        through = None
        for level in range(depth_count):
            values = samples_ref[level, :, lanes].astype(jnp.float32)
            extinction = EXTINCTION * values
            before = extinction if before is None else before + extinction
            after = jnp.exp(-before)
            weight = (1.0 - after) if through is None else (through - after)
            through = after
            absent = 1.0 / (1.0 + values)
            red = weight * (1.0 - absent)
            green = red * absent
            if level == 0:
                red_sum, green_sum = red, green
            else:
                red_sum, green_sum = red_sum + red, green_sum + green
        out_ref[part, 0, 0] = red_sum
        out_ref[part, 0, 1] = 4.0 * green_sum
        out_ref[part, 0, 2] = before


def render_chunks(levels, group_count, swap_count):
    depth_count, per_device, pixels = levels.shape
    parts = 4
    return pl.pallas_call(
        render_kernel,
        grid=(pixels // (parts * LANES),),
        in_specs=[pl.BlockSpec((depth_count, per_device, parts * LANES), lambda i: (0, 0, i))],
        out_specs=pl.BlockSpec(
            (parts, 1, 3, per_device, LANES),
            lambda i: (i % (group_count // parts), i // (group_count // parts), 0, 0, 0),
        ),
        out_shape=jax.ShapeDtypeStruct(
            (group_count, swap_count, 3, per_device, LANES), jnp.float32
        ),
        compiler_params=pltpu.CompilerParams(vmem_limit_bytes=VMEM_BYTES),
    )(levels)


def mask_kernel(key_count, tiles_ref, keys_ref, slots_ref, front_ref, member_ref):
    swap_count, fragment_count = tiles_ref.shape
    slot_count = slots_ref.shape[1]
    slot_id = lax.broadcasted_iota(jnp.int32, (slot_count, slot_count), 0).astype(jnp.float32)
    tile_id = lax.broadcasted_iota(jnp.int32, (slot_count, slot_count), 1).astype(jnp.float32)
    held = jnp.where(slots_ref[...] == slot_id, tile_id, 0.0)
    slot_tile = jnp.sum(held, axis=1, keepdims=True)
    for slab in range(swap_count):
        tiles = tiles_ref[slab : slab + 1, :]
        codes = tiles * float(key_count) + keys_ref[slab : slab + 1, :]
        member_ref[slab] = jnp.where(tiles == slot_tile, 1.0, 0.0).astype(jnp.bfloat16)
        for start in range(0, fragment_count, LANES):
            block = slice(start, start + LANES)
            mine = jnp.broadcast_to(codes[:, block], (LANES, LANES)).T
            least = jnp.broadcast_to(tiles[:, block], (LANES, LANES)).T * float(key_count)
            for other in range(0, fragment_count, LANES):
                theirs = codes[:, other : other + LANES]
                nearer = (theirs >= least) & (theirs < mine)
                front_ref[slab, block, other : other + LANES] = jnp.where(
                    nearer, 1.0, 0.0
                ).astype(jnp.bfloat16)


def depth_masks(tile_list, tile_slot, brick_rank):
    swap_count, group_count, per_device = tile_list.shape
    fragment_count = group_count * per_device
    slot_count = tile_slot.shape[0]
    key_count = brick_rank.shape[1]
    tiles = tile_list.reshape(swap_count, fragment_count).astype(jnp.float32)
    keys = jnp.broadcast_to(
        brick_rank[:, :, None], (swap_count, key_count, fragment_count // key_count)
    )
    keys = keys.reshape(swap_count, fragment_count).astype(jnp.float32)
    return pl.pallas_call(
        functools.partial(mask_kernel, key_count),
        out_shape=[
            jax.ShapeDtypeStruct((swap_count, fragment_count, fragment_count), jnp.bfloat16),
            jax.ShapeDtypeStruct((swap_count, slot_count, fragment_count), jnp.bfloat16),
        ],
        compiler_params=pltpu.CompilerParams(vmem_limit_bytes=VMEM_BYTES),
    )(tiles, keys, tile_slot.astype(jnp.float32)[None])


def split(values):
    high = values.astype(jnp.bfloat16)
    low = (values - high.astype(jnp.float32)).astype(jnp.bfloat16)
    return jnp.concatenate([high, low], axis=1)


def masked_sum(mask, values):
    both = jnp.dot(mask, split(values), preferred_element_type=jnp.float32)
    width = values.shape[1]
    return both[:, :width] + both[:, width:]


def composite_kernel(chunk_ref, front_ref, member_ref, out_ref):
    group_count, swap_count, _, per_device, lanes = chunk_ref.shape
    shape = (group_count * per_device, lanes)
    for slab in range(swap_count):
        optical = chunk_ref[:, slab, 2].reshape(shape)
        through = jnp.exp(-masked_sum(front_ref[slab], optical))
        red = chunk_ref[:, slab, 0].reshape(shape) * through
        green = chunk_ref[:, slab, 1].reshape(shape) * through
        sums = masked_sum(member_ref[slab], jnp.concatenate([red, green, optical], axis=1))
        if slab == 0:
            colors, depth = sums[:, : 2 * lanes], sums[:, 2 * lanes :]
        else:
            seen = jnp.exp(-depth)
            colors = colors + jnp.concatenate([seen, seen], axis=1) * sums[:, : 2 * lanes]
            depth = depth + sums[:, 2 * lanes :]
    owned = out_ref.shape[2]
    tiles = (group_count, owned, lanes)
    out_ref[:, 0] = colors[:, :lanes].reshape(tiles)
    out_ref[:, 1] = colors[:, lanes:].reshape(tiles)
    out_ref[:, 2] = (1.0 - jnp.exp(-depth)).reshape(tiles)


def composite(chunk, front, member):
    group_count, _, _, _, lanes = chunk.shape
    owned = member.shape[1] // group_count
    return pl.pallas_call(
        composite_kernel,
        out_shape=jax.ShapeDtypeStruct((group_count, 3, owned, lanes), jnp.float32),
        compiler_params=pltpu.CompilerParams(vmem_limit_bytes=VMEM_BYTES),
    )(chunk, front, member)


def chunk_shards(samples, tile_list, tile_slot, brick_rank):
    group_count = lax.axis_size("grp")
    swap_count = lax.axis_size("swap")
    per_device, pixels = samples.shape[2], samples.shape[4]
    owned = tile_slot.shape[0] // group_count
    levels = jnp.transpose(samples[0, 0], (1, 0, 2))
    leaving = render_chunks(levels, group_count, swap_count)
    arrived = lax.all_to_all(
        leaving.reshape(group_count * swap_count, 3, per_device, LANES),
        ("grp", "swap"),
        split_axis=0,
        concat_axis=0,
        tiled=True,
    )
    front, member = depth_masks(tile_list, tile_slot, brick_rank)
    tiles = composite(
        arrived.reshape(group_count, swap_count, 3, per_device, LANES), front, member
    )
    image = lax.all_to_all(tiles, "grp", split_axis=0, concat_axis=0, tiled=True)
    red, green, opacity = (
        jnp.transpose(image[:, channel], (1, 0, 2)).reshape(owned, pixels // swap_count)
        for channel in range(3)
    )
    return jnp.stack([red, green, opacity - red, opacity], axis=1)[None]


def shards(samples, tile_list, tile_slot, brick_rank):
    device_count = lax.axis_size("grp") * lax.axis_size("swap")
    fragment_count = tile_list.shape[1] * tile_list.shape[2]
    if samples.shape[4] == device_count * LANES and fragment_count <= 1024:
        return chunk_shards(samples, tile_list, tile_slot, brick_rank)
    return general_shards(samples, tile_list, tile_slot, brick_rank)


def solution(mesh):
    return jax.shard_map(
        shards,
        mesh=mesh,
        in_specs=(P("swap", "grp", None, None, None), P(), P(), P()),
        out_specs=P("grp", None, None, "swap"),
        check_vma=False,
    )
```

```python
import functools
import jax
import jax.numpy as jnp
from jax import lax
from jax.experimental import pallas as pl
from jax.experimental.pallas import tpu as pltpu
from jax.sharding import PartitionSpec as P

BRICKS = 8


EXTINCTION = 0.024


def from_partner(array, axis, apart):
    return lax.ppermute(array, axis, [(i, i ^ 1 << apart) for i in range(lax.axis_size(axis))])


def render(values_in):
    depth_count = values_in.shape[1]
    shape = (values_in.shape[0], values_in.shape[2])
    before = jnp.zeros(shape, jnp.float32)
    red_sum = jnp.zeros(shape, jnp.float32)
    green_sum = jnp.zeros(shape, jnp.float32)
    blue_sum = jnp.zeros(shape, jnp.float32)
    for level in range(depth_count):
        values = values_in[:, level].astype(jnp.float32)
        extinction = EXTINCTION * values
        weight = jnp.exp(-before) * (1.0 - jnp.exp(-extinction))
        ratio = values / (1.0 + values)
        red_sum = red_sum + weight * ratio
        green_sum = green_sum + weight * 4.0 * ratio * (1.0 - ratio)
        blue_sum = blue_sum + weight * (1.0 - ratio)
        before = before + extinction
    return jnp.stack([red_sum, green_sum, blue_sum, before], axis=1)


def over_pair(front_part, back_part):
    colors = front_part[:, :3] + jnp.exp(-front_part[:, 3:4]) * back_part[:, :3]
    return jnp.concatenate([colors, front_part[:, 3:4] + back_part[:, 3:4]], axis=1)


def slot_tables(tiles_in, tile_slot, owned, per_brick, ranks_in):
    group_count, per_device = tiles_in.shape
    slot_ids = tile_slot[tiles_in]
    owners = slot_ids // owned
    tile_rows = slot_ids % owned
    position = jnp.arange(per_device, dtype=jnp.int32)
    same_owner = (owners[:, :, None] == owners[:, None, :]) & (
        position[None, None, :] < position[None, :, None]
    )
    places = jnp.sum(same_owner.astype(jnp.int32), axis=2)
    depth_keys = jnp.repeat(ranks_in.reshape(group_count, BRICKS), per_brick, axis=1)
    return (owners, tile_rows, places, depth_keys)


def arrivals(owners, tile_rows, places, depth_keys, device, capacity):
    slot_ids = jnp.arange(capacity, dtype=jnp.int32)
    matched = (
        (owners[:, None, :] == device) & (places[:, None, :] == slot_ids[None, :, None])
    ).astype(jnp.int32)
    rows_in = jnp.sum(matched * tile_rows[:, None, :], axis=2).reshape(-1)
    keys_in = jnp.sum(matched * depth_keys[:, None, :], axis=2).reshape(-1)
    valid_in = (jnp.sum(matched, axis=2) > 0).reshape(-1)
    return (rows_in, keys_in, valid_in)


def outgoing(fragments, owners_mine, places_mine, group_count, capacity):
    per_device = fragments.shape[0]
    target = owners_mine * capacity + places_mine
    slot_ids = jnp.arange(group_count * capacity, dtype=jnp.int32)
    matched = (target[None, :] == slot_ids[:, None]).astype(jnp.int32)
    numbers = jnp.arange(per_device, dtype=jnp.int32) + 1
    source = jnp.sum(matched * numbers[None, :], axis=1) - 1
    source = jnp.where(source < 0, per_device, source)
    padded = jnp.concatenate(
        [fragments, jnp.zeros((1,) + fragments.shape[1:], jnp.float32)], axis=0
    )
    return jnp.take(padded, source, axis=0)


def combine(pieces, rows_in, keys_in, valid_in, owned):
    optical = pieces[:, 3]
    both_valid = valid_in[:, None] & valid_in[None, :]
    in_front = (
        (rows_in[:, None] == rows_in[None, :]) & both_valid & (keys_in[None, :] < keys_in[:, None])
    ).astype(jnp.float32)
    prefix = jnp.dot(
        in_front, optical, precision=lax.Precision.HIGHEST, preferred_element_type=jnp.float32
    )
    shaded = pieces[:, :3] * jnp.exp(-prefix)[:, None]
    to_rows = (
        (jnp.arange(owned, dtype=jnp.int32)[:, None] == rows_in[None, :]) & valid_in[None, :]
    ).astype(jnp.float32)
    colors = jnp.einsum("of,fcp->ocp", to_rows, shaded, precision=lax.Precision.HIGHEST)
    summed = jnp.dot(
        to_rows, optical, precision=lax.Precision.HIGHEST, preferred_element_type=jnp.float32
    )
    return jnp.concatenate([colors, summed[:, None]], axis=1)


def leaving_of(fragments, owners_slab, places_slab, device, group_count, capacity):
    owners_mine = lax.dynamic_index_in_dim(owners_slab, device, 0, keepdims=False)
    places_mine = lax.dynamic_index_in_dim(places_slab, device, 0, keepdims=False)
    return outgoing(fragments, owners_mine, places_mine, group_count, capacity)


def general_shards(samples, tile_list, tile_slot, brick_rank):
    group_count = lax.axis_size("grp")
    swap_count = lax.axis_size("swap")
    device = lax.axis_index("grp")
    slab = lax.axis_index("swap")
    per_device = tile_list.shape[2]
    per_brick = per_device // BRICKS
    owned = tile_slot.shape[0] // group_count
    capacity = 2 * per_device // group_count
    pixels = samples.shape[4]
    block = pixels // swap_count
    fragments = render(samples[0, 0])
    tiles_slab = lax.dynamic_index_in_dim(tile_list, slab, 0, keepdims=False)
    ranks_slab = lax.dynamic_index_in_dim(brick_rank, slab, 0, keepdims=False)
    owners_slab, rows_slab, places_slab, keys_slab = slot_tables(
        tiles_slab, tile_slot, owned, per_brick, ranks_slab
    )
    leaving = leaving_of(fragments, owners_slab, places_slab, device, group_count, capacity)
    rows_in, keys_in, valid_in = arrivals(
        owners_slab, rows_slab, places_slab, keys_slab, device, capacity
    )
    arrived = lax.all_to_all(
        leaving.reshape(group_count, capacity, 4, pixels),
        "grp",
        split_axis=0,
        concat_axis=0,
        tiled=True,
    )
    partial_value = combine(
        arrived.reshape(-1, 4, arrived.shape[3]), rows_in, keys_in, valid_in, owned
    )
    levels = swap_count.bit_length() - 1
    partial_value = partial_value.reshape((owned, 4) + (2,) * levels + (block,))
    for level in range(levels):
        lower = partial_value[..., 0, :]
        upper = partial_value[..., 1, :]
        my_bit = jnp.right_shift(slab, level) % 2
        kept = jnp.where(my_bit == 1, upper, lower)
        given = jnp.where(my_bit == 1, lower, upper)
        received = from_partner(given, "swap", level)
        front_part = jnp.where(my_bit == 0, kept, received)
        back_part = jnp.where(my_bit == 0, received, kept)
        partial_value = over_pair(front_part, back_part)
    final_image = jnp.concatenate(
        [partial_value[:, :3], 1.0 - jnp.exp(-partial_value[:, 3:4])], axis=1
    )
    return final_image[None]


LANES = 128
VMEM_BYTES = 20 * 1024 * 1024


def level_order(fragments, depth_count):
    rows = fragments * depth_count
    to = lax.broadcasted_iota(jnp.int32, (rows, rows), 0)
    source = lax.broadcasted_iota(jnp.int32, (rows, rows), 1)
    wanted = (to % fragments) * depth_count + to // fragments
    return jnp.where(source == wanted, 1.0, 0.0).astype(jnp.bfloat16)


def render_levels(levels):
    before = through = held = held_twice = None
    for level in range(levels.shape[0]):
        values = levels[level]
        extinction = EXTINCTION * values
        before = extinction if before is None else before + extinction
        after = jnp.exp(-before)
        weight = (1.0 - after) if through is None else (through - after)
        through = after
        absent = 1.0 / (1.0 + values)
        once = weight * absent
        twice = once * absent
        held = once if held is None else held + once
        held_twice = twice if held_twice is None else held_twice + twice
    return (1.0 - through) - held, 4.0 * (held - held_twice), before


def render_kernel(samples_ref, out_ref, held_ref, made_ref, in_sems, out_sems):
    group_count, swap_count = out_ref.shape[:2]
    fragments, depth_count, pixels = samples_ref.shape
    pieces, width = held_ref.shape[0], held_ref.shape[3]
    chunks = width // LANES
    per_slab = group_count // chunks
    arriving, leaving = [], []
    for piece in range(pieces):
        part = samples_ref.at[:, :, pl.ds(piece * width, width)]
        arriving.append(pltpu.make_async_copy(part, held_ref.at[piece], in_sems.at[piece]))
        place = (pl.ds(piece % per_slab * chunks, chunks), piece // per_slab)
        leaving.append(
            pltpu.make_async_copy(made_ref.at[place], out_ref.at[place], out_sems.at[piece])
        )
    for copy in arriving:
        copy.start()
    order = level_order(fragments, depth_count)
    for piece in range(pieces):
        arriving[piece].wait()
        levels = jnp.dot(
            order,
            held_ref[piece].reshape(fragments * depth_count, width),
            preferred_element_type=jnp.float32,
        ).reshape(depth_count, fragments, width)
        for at in range(chunks):
            channels = render_levels(levels[:, :, at * LANES : (at + 1) * LANES])
            chunk = piece % per_slab * chunks + at
            for channel in range(3):
                made_ref[chunk, piece // per_slab, channel] = channels[channel]
        leaving[piece].start()
    for copy in leaving:
        copy.wait()


def render_chunks(samples, group_count, swap_count):
    fragments, depth_count, pixels = samples.shape
    pieces = 4
    out_shape = (group_count, swap_count, 3, fragments, LANES)
    return pl.pallas_call(
        render_kernel,
        in_specs=[pl.BlockSpec(memory_space=pltpu.HBM)],
        out_specs=pl.BlockSpec(memory_space=pltpu.HBM),
        out_shape=jax.ShapeDtypeStruct(out_shape, jnp.float32),
        scratch_shapes=[
            pltpu.VMEM((pieces, fragments, depth_count, pixels // pieces), jnp.bfloat16),
            pltpu.VMEM(out_shape, jnp.float32),
            pltpu.SemaphoreType.DMA((pieces,)),
            pltpu.SemaphoreType.DMA((pieces,)),
        ],
        compiler_params=pltpu.CompilerParams(vmem_limit_bytes=3 * VMEM_BYTES),
    )(pltpu.with_memory_space_constraint(samples, pltpu.HBM))


def split(values):
    high = values.astype(jnp.bfloat16)
    low = (values - high.astype(jnp.float32)).astype(jnp.bfloat16)
    return jnp.concatenate([high, low], axis=1)


def masked_sum(mask, parts):
    both = jnp.dot(mask, parts, preferred_element_type=jnp.float32)
    width = parts.shape[1] // 2
    return both[:, :width] + both[:, width:]


def composite_kernel(order_ref, chunk_ref, member_ref, back_ref, out_ref, *scratch):
    member_held, back_held, sorted_ref, sems = scratch
    group_count, swap_count, channels, per_device, lanes = chunk_ref.shape
    copies = [
        pltpu.make_async_copy(member_ref, member_held, sems.at[0]),
        pltpu.make_async_copy(back_ref, back_held, sems.at[1]),
    ]
    for copy in copies:
        copy.start()
    per_brick = per_device // BRICKS
    bricks = group_count * BRICKS
    for at in range(swap_count * bricks):
        brick = order_ref[at]
        source = lax.div(brick, BRICKS)
        first = pl.multiple_of(lax.rem(brick, BRICKS) * per_brick, per_brick)
        for channel in range(channels):
            sorted_ref[
                at * per_brick : (at + 1) * per_brick, channel * lanes : (channel + 1) * lanes
            ] = chunk_ref[source, at // bricks, channel, pl.ds(first, per_brick), :]
    for copy in copies:
        copy.wait()
    fragment_count = swap_count * bricks * per_brick
    block = min(2 * LANES, fragment_count)
    starts = range(0, fragment_count, block)
    row = lax.broadcasted_iota(jnp.int32, (block, block), 0) // per_brick
    column = lax.broadcasted_iota(jnp.int32, (block, block), 1) // per_brick
    nearer = column < row
    members = [member_held[:, start : start + block] for start in starts]
    backs = [back_held[start : start + block, :] for start in starts]
    opticals = [split(sorted_ref[start : start + block, 2 * lanes :]) for start in starts]
    added = [masked_sum(member, optical) for member, optical in zip(members, opticals)]
    fronts = []
    for member, back in zip(members, backs):
        same = jnp.dot(back, member, preferred_element_type=jnp.float32)
        fronts.append(jnp.where(nearer, same, 0.0).astype(jnp.bfloat16))
    depths = [added[0]]
    for value in added[1:]:
        depths.append(depths[-1] + value)
    throughs = []
    for at, (front, back, optical) in enumerate(zip(fronts, backs, opticals)):
        before = masked_sum(front, optical)
        if at > 0:
            before = before + masked_sum(back, split(depths[at - 1]))
        throughs.append(jnp.exp(-before))
    color = None
    for start, member, through in zip(starts, members, throughs):
        both = jnp.concatenate([through, through], axis=1)
        shaded = split(sorted_ref[start : start + block, : 2 * lanes] * both)
        shaded = masked_sum(member, shaded)
        color = shaded if color is None else color + shaded
    owned = out_ref.shape[2]
    tiles = (group_count, owned, lanes)
    out_ref[:, 0] = color[:, :lanes].reshape(tiles)
    out_ref[:, 1] = color[:, lanes:].reshape(tiles)
    out_ref[:, 2] = (1.0 - jnp.exp(-depths[-1])).reshape(tiles)


def composite(order, chunk, member, back):
    group_count, swap_count, channels, per_device, lanes = chunk.shape
    slot_count, fragment_count = member.shape
    return pl.pallas_call(
        composite_kernel,
        in_specs=[
            pl.BlockSpec(memory_space=pltpu.SMEM),
            pl.BlockSpec(memory_space=pltpu.VMEM),
            pl.BlockSpec(memory_space=pltpu.HBM),
            pl.BlockSpec(memory_space=pltpu.HBM),
        ],
        out_specs=pl.BlockSpec(memory_space=pltpu.VMEM),
        out_shape=jax.ShapeDtypeStruct(
            (group_count, channels, slot_count // group_count, lanes), jnp.float32
        ),
        scratch_shapes=[
            pltpu.VMEM(member.shape, member.dtype),
            pltpu.VMEM(back.shape, back.dtype),
            pltpu.VMEM((fragment_count, channels * lanes), jnp.float32),
            pltpu.SemaphoreType.DMA((2,)),
        ],
        compiler_params=pltpu.CompilerParams(vmem_limit_bytes=VMEM_BYTES),
    )(
        order,
        chunk,
        pltpu.with_memory_space_constraint(member, pltpu.HBM),
        pltpu.with_memory_space_constraint(back, pltpu.HBM),
    )


def depth_order(tile_list, tile_slot, brick_rank):
    swap_count, brick_count = brick_rank.shape
    numbers = jnp.arange(brick_count, dtype=jnp.int32)
    placed = brick_rank[:, None, :] == numbers[None, :, None]
    order = jnp.sum(jnp.where(placed, numbers[None, None, :], 0), axis=2)
    slot_count = tile_slot.shape[0]
    ids = jnp.arange(slot_count, dtype=jnp.int32)
    found = tile_list[..., None] == ids
    slots = jnp.sum(jnp.where(found, tile_slot, 0), axis=-1)
    slots = slots.reshape(swap_count, 1, brick_count, -1)
    slots = jnp.sum(jnp.where(placed[..., None], slots, 0), axis=2).reshape(-1)
    member = (ids[:, None] == slots[None, :]).astype(jnp.bfloat16)
    back = (slots[:, None] == ids[None, :]).astype(jnp.bfloat16)
    return order.reshape(-1), member, back


def chunk_shards(samples, tile_list, tile_slot, brick_rank):
    group_count = lax.axis_size("grp")
    swap_count = lax.axis_size("swap")
    per_device, pixels = samples.shape[2], samples.shape[4]
    owned = tile_slot.shape[0] // group_count
    leaving = render_chunks(samples[0, 0], group_count, swap_count)
    arrived = lax.all_to_all(
        leaving.reshape(group_count * swap_count, 3, per_device, LANES),
        ("grp", "swap"),
        split_axis=0,
        concat_axis=0,
        tiled=True,
    )
    order, member, back = depth_order(tile_list, tile_slot, brick_rank)
    tiles = composite(
        order, arrived.reshape(group_count, swap_count, 3, per_device, LANES), member, back
    )
    image = lax.all_to_all(tiles, "grp", split_axis=0, concat_axis=0, tiled=True)
    red, green, opacity = (
        jnp.transpose(image[:, channel], (1, 0, 2)).reshape(owned, pixels // swap_count)
        for channel in range(3)
    )
    return jnp.stack([red, green, opacity - red, opacity], axis=1)[None]


def shards(samples, tile_list, tile_slot, brick_rank):
    device_count = lax.axis_size("grp") * lax.axis_size("swap")
    fragment_count = tile_list.shape[1] * tile_list.shape[2]
    if samples.shape[4] == device_count * LANES and fragment_count <= 1024:
        return chunk_shards(samples, tile_list, tile_slot, brick_rank)
    return general_shards(samples, tile_list, tile_slot, brick_rank)


def solution(mesh):
    return jax.shard_map(
        shards,
        mesh=mesh,
        in_specs=(P("swap", "grp", None, None, None), P(), P(), P()),
        out_specs=P("grp", None, None, "swap"),
        check_vma=False,
    )
```

```python
import functools
import jax
import jax.numpy as jnp
from jax import lax
from jax.experimental import pallas as pl
from jax.experimental.pallas import tpu as pltpu
from jax.sharding import PartitionSpec as P

BRICKS = 8


EXTINCTION = 0.024


def from_partner(array, axis, apart):
    return lax.ppermute(array, axis, [(i, i ^ 1 << apart) for i in range(lax.axis_size(axis))])


def render(values_in):
    depth_count = values_in.shape[1]
    shape = (values_in.shape[0], values_in.shape[2])
    before = jnp.zeros(shape, jnp.float32)
    red_sum = jnp.zeros(shape, jnp.float32)
    green_sum = jnp.zeros(shape, jnp.float32)
    blue_sum = jnp.zeros(shape, jnp.float32)
    for level in range(depth_count):
        values = values_in[:, level].astype(jnp.float32)
        extinction = EXTINCTION * values
        weight = jnp.exp(-before) * (1.0 - jnp.exp(-extinction))
        ratio = values / (1.0 + values)
        red_sum = red_sum + weight * ratio
        green_sum = green_sum + weight * 4.0 * ratio * (1.0 - ratio)
        blue_sum = blue_sum + weight * (1.0 - ratio)
        before = before + extinction
    return jnp.stack([red_sum, green_sum, blue_sum, before], axis=1)


def over_pair(front_part, back_part):
    colors = front_part[:, :3] + jnp.exp(-front_part[:, 3:4]) * back_part[:, :3]
    return jnp.concatenate([colors, front_part[:, 3:4] + back_part[:, 3:4]], axis=1)


def slot_tables(tiles_in, tile_slot, owned, per_brick, ranks_in):
    group_count, per_device = tiles_in.shape
    slot_ids = tile_slot[tiles_in]
    owners = slot_ids // owned
    tile_rows = slot_ids % owned
    position = jnp.arange(per_device, dtype=jnp.int32)
    same_owner = (owners[:, :, None] == owners[:, None, :]) & (
        position[None, None, :] < position[None, :, None]
    )
    places = jnp.sum(same_owner.astype(jnp.int32), axis=2)
    depth_keys = jnp.repeat(ranks_in.reshape(group_count, BRICKS), per_brick, axis=1)
    return (owners, tile_rows, places, depth_keys)


def arrivals(owners, tile_rows, places, depth_keys, device, capacity):
    slot_ids = jnp.arange(capacity, dtype=jnp.int32)
    matched = (
        (owners[:, None, :] == device) & (places[:, None, :] == slot_ids[None, :, None])
    ).astype(jnp.int32)
    rows_in = jnp.sum(matched * tile_rows[:, None, :], axis=2).reshape(-1)
    keys_in = jnp.sum(matched * depth_keys[:, None, :], axis=2).reshape(-1)
    valid_in = (jnp.sum(matched, axis=2) > 0).reshape(-1)
    return (rows_in, keys_in, valid_in)


def outgoing(fragments, owners_mine, places_mine, group_count, capacity):
    per_device = fragments.shape[0]
    target = owners_mine * capacity + places_mine
    slot_ids = jnp.arange(group_count * capacity, dtype=jnp.int32)
    matched = (target[None, :] == slot_ids[:, None]).astype(jnp.int32)
    numbers = jnp.arange(per_device, dtype=jnp.int32) + 1
    source = jnp.sum(matched * numbers[None, :], axis=1) - 1
    source = jnp.where(source < 0, per_device, source)
    padded = jnp.concatenate(
        [fragments, jnp.zeros((1,) + fragments.shape[1:], jnp.float32)], axis=0
    )
    return jnp.take(padded, source, axis=0)


def combine(pieces, rows_in, keys_in, valid_in, owned):
    optical = pieces[:, 3]
    both_valid = valid_in[:, None] & valid_in[None, :]
    in_front = (
        (rows_in[:, None] == rows_in[None, :]) & both_valid & (keys_in[None, :] < keys_in[:, None])
    ).astype(jnp.float32)
    prefix = jnp.dot(
        in_front, optical, precision=lax.Precision.HIGHEST, preferred_element_type=jnp.float32
    )
    shaded = pieces[:, :3] * jnp.exp(-prefix)[:, None]
    to_rows = (
        (jnp.arange(owned, dtype=jnp.int32)[:, None] == rows_in[None, :]) & valid_in[None, :]
    ).astype(jnp.float32)
    colors = jnp.einsum("of,fcp->ocp", to_rows, shaded, precision=lax.Precision.HIGHEST)
    summed = jnp.dot(
        to_rows, optical, precision=lax.Precision.HIGHEST, preferred_element_type=jnp.float32
    )
    return jnp.concatenate([colors, summed[:, None]], axis=1)


def leaving_of(fragments, owners_slab, places_slab, device, group_count, capacity):
    owners_mine = lax.dynamic_index_in_dim(owners_slab, device, 0, keepdims=False)
    places_mine = lax.dynamic_index_in_dim(places_slab, device, 0, keepdims=False)
    return outgoing(fragments, owners_mine, places_mine, group_count, capacity)


def general_shards(samples, tile_list, tile_slot, brick_rank):
    group_count = lax.axis_size("grp")
    swap_count = lax.axis_size("swap")
    device = lax.axis_index("grp")
    slab = lax.axis_index("swap")
    per_device = tile_list.shape[2]
    per_brick = per_device // BRICKS
    owned = tile_slot.shape[0] // group_count
    capacity = 2 * per_device // group_count
    pixels = samples.shape[4]
    block = pixels // swap_count
    fragments = render(samples[0, 0])
    tiles_slab = lax.dynamic_index_in_dim(tile_list, slab, 0, keepdims=False)
    ranks_slab = lax.dynamic_index_in_dim(brick_rank, slab, 0, keepdims=False)
    owners_slab, rows_slab, places_slab, keys_slab = slot_tables(
        tiles_slab, tile_slot, owned, per_brick, ranks_slab
    )
    leaving = leaving_of(fragments, owners_slab, places_slab, device, group_count, capacity)
    rows_in, keys_in, valid_in = arrivals(
        owners_slab, rows_slab, places_slab, keys_slab, device, capacity
    )
    arrived = lax.all_to_all(
        leaving.reshape(group_count, capacity, 4, pixels),
        "grp",
        split_axis=0,
        concat_axis=0,
        tiled=True,
    )
    partial_value = combine(
        arrived.reshape(-1, 4, arrived.shape[3]), rows_in, keys_in, valid_in, owned
    )
    levels = swap_count.bit_length() - 1
    partial_value = partial_value.reshape((owned, 4) + (2,) * levels + (block,))
    for level in range(levels):
        lower = partial_value[..., 0, :]
        upper = partial_value[..., 1, :]
        my_bit = jnp.right_shift(slab, level) % 2
        kept = jnp.where(my_bit == 1, upper, lower)
        given = jnp.where(my_bit == 1, lower, upper)
        received = from_partner(given, "swap", level)
        front_part = jnp.where(my_bit == 0, kept, received)
        back_part = jnp.where(my_bit == 0, received, kept)
        partial_value = over_pair(front_part, back_part)
    final_image = jnp.concatenate(
        [partial_value[:, :3], 1.0 - jnp.exp(-partial_value[:, 3:4])], axis=1
    )
    return final_image[None]


LANES = 128
VMEM_BYTES = 20 * 1024 * 1024


def level_order(fragments, depth_count):
    rows = fragments * depth_count
    to = lax.broadcasted_iota(jnp.int32, (rows, rows), 0)
    source = lax.broadcasted_iota(jnp.int32, (rows, rows), 1)
    wanted = (to % fragments) * depth_count + to // fragments
    return jnp.where(source == wanted, 1.0, 0.0).astype(jnp.bfloat16)


def render_levels(levels):
    before = through = held = held_twice = None
    for level in range(levels.shape[0]):
        values = levels[level]
        extinction = EXTINCTION * values
        before = extinction if before is None else before + extinction
        after = jnp.exp(-before)
        weight = (1.0 - after) if through is None else (through - after)
        through = after
        absent = 1.0 / (1.0 + values)
        once = weight * absent
        twice = once * absent
        held = once if held is None else held + once
        held_twice = twice if held_twice is None else held_twice + twice
    return (1.0 - through) - held, 4.0 * (held - held_twice), before


def render_kernel(samples_ref, out_ref, held_ref, made_ref, in_sems, out_sems):
    group_count, swap_count = out_ref.shape[:2]
    fragments, depth_count, pixels = samples_ref.shape
    pieces, width = held_ref.shape[0], held_ref.shape[3]
    chunks = width // LANES
    per_slab = group_count // chunks
    arriving, leaving = [], []
    for piece in range(pieces):
        part = samples_ref.at[:, :, pl.ds(piece * width, width)]
        arriving.append(pltpu.make_async_copy(part, held_ref.at[piece], in_sems.at[piece]))
        place = (pl.ds(piece % per_slab * chunks, chunks), piece // per_slab)
        leaving.append(
            pltpu.make_async_copy(made_ref.at[place], out_ref.at[place], out_sems.at[piece])
        )
    for copy in arriving:
        copy.start()
    order = level_order(fragments, depth_count)
    for piece in range(pieces):
        arriving[piece].wait()
        levels = jnp.dot(
            order,
            held_ref[piece].reshape(fragments * depth_count, width),
            preferred_element_type=jnp.float32,
        ).reshape(depth_count, fragments, width)
        for at in range(chunks):
            channels = render_levels(levels[:, :, at * LANES : (at + 1) * LANES])
            chunk = piece % per_slab * chunks + at
            for channel in range(3):
                made_ref[chunk, piece // per_slab, channel] = channels[channel]
        leaving[piece].start()
    for copy in leaving:
        copy.wait()


def render_chunks(samples, group_count, swap_count):
    fragments, depth_count, pixels = samples.shape
    pieces = 4
    out_shape = (group_count, swap_count, 3, fragments, LANES)
    return pl.pallas_call(
        render_kernel,
        in_specs=[pl.BlockSpec(memory_space=pltpu.HBM)],
        out_specs=pl.BlockSpec(memory_space=pltpu.HBM),
        out_shape=jax.ShapeDtypeStruct(out_shape, jnp.float32),
        scratch_shapes=[
            pltpu.VMEM((pieces, fragments, depth_count, pixels // pieces), jnp.bfloat16),
            pltpu.VMEM(out_shape, jnp.float32),
            pltpu.SemaphoreType.DMA((pieces,)),
            pltpu.SemaphoreType.DMA((pieces,)),
        ],
        compiler_params=pltpu.CompilerParams(vmem_limit_bytes=3 * VMEM_BYTES),
    )(pltpu.with_memory_space_constraint(samples, pltpu.HBM))


def split(values):
    high = values.astype(jnp.bfloat16)
    low = (values - high.astype(jnp.float32)).astype(jnp.bfloat16)
    return jnp.concatenate([high, low], axis=1)


def masked_sum(mask, parts):
    both = jnp.dot(mask, parts, preferred_element_type=jnp.float32)
    width = parts.shape[1] // 2
    return both[:, :width] + both[:, width:]


def composite_kernel(order_ref, chunk_ref, slots_ref, out_ref, sorted_ref):
    group_count, swap_count, channels, per_device, lanes = chunk_ref.shape
    per_brick = per_device // BRICKS
    bricks = group_count * BRICKS
    for at in range(swap_count * bricks):
        brick = order_ref[at]
        source = lax.div(brick, BRICKS)
        first = pl.multiple_of(lax.rem(brick, BRICKS) * per_brick, per_brick)
        for channel in range(channels):
            sorted_ref[
                at * per_brick : (at + 1) * per_brick, channel * lanes : (channel + 1) * lanes
            ] = chunk_ref[source, at // bricks, channel, pl.ds(first, per_brick), :]
    fragment_count = swap_count * bricks * per_brick
    block = min(2 * LANES, fragment_count)
    starts = range(0, fragment_count, block)
    row = lax.broadcasted_iota(jnp.int32, (block, block), 0) // per_brick
    column = lax.broadcasted_iota(jnp.int32, (block, block), 1) // per_brick
    nearer = column < row
    slot_count = group_count * out_ref.shape[2]
    slot_id = lax.broadcasted_iota(jnp.int32, (slot_count, block), 0).astype(jnp.float32)
    members, backs = [], []
    for start in starts:
        found = jnp.where(slots_ref[:, start : start + block] == slot_id, 1.0, 0.0)
        members.append(found.astype(jnp.bfloat16))
        backs.append(found.T.astype(jnp.bfloat16))
    opticals = [split(sorted_ref[start : start + block, 2 * lanes :]) for start in starts]
    added = [masked_sum(member, optical) for member, optical in zip(members, opticals)]
    fronts = []
    for member, back in zip(members, backs):
        same = jnp.dot(back, member, preferred_element_type=jnp.float32)
        fronts.append(jnp.where(nearer, same, 0.0).astype(jnp.bfloat16))
    depths = [added[0]]
    for value in added[1:]:
        depths.append(depths[-1] + value)
    throughs = []
    for at, (front, back, optical) in enumerate(zip(fronts, backs, opticals)):
        before = masked_sum(front, optical)
        if at > 0:
            before = before + masked_sum(back, split(depths[at - 1]))
        throughs.append(jnp.exp(-before))
    color = None
    for start, member, through in zip(starts, members, throughs):
        both = jnp.concatenate([through, through], axis=1)
        shaded = split(sorted_ref[start : start + block, : 2 * lanes] * both)
        shaded = masked_sum(member, shaded)
        color = shaded if color is None else color + shaded
    owned = out_ref.shape[2]
    tiles = (group_count, owned, lanes)
    out_ref[:, 0] = color[:, :lanes].reshape(tiles)
    out_ref[:, 1] = color[:, lanes:].reshape(tiles)
    out_ref[:, 2] = (1.0 - jnp.exp(-depths[-1])).reshape(tiles)


def composite(order, chunk, slots, slot_count):
    group_count, _, channels, _, lanes = chunk.shape
    vmem = pl.BlockSpec(memory_space=pltpu.VMEM)
    return pl.pallas_call(
        composite_kernel,
        in_specs=[pl.BlockSpec(memory_space=pltpu.SMEM), vmem, vmem],
        out_specs=vmem,
        out_shape=jax.ShapeDtypeStruct(
            (group_count, channels, slot_count // group_count, lanes), jnp.float32
        ),
        scratch_shapes=[pltpu.VMEM((slots.shape[1], channels * lanes), jnp.float32)],
        compiler_params=pltpu.CompilerParams(vmem_limit_bytes=VMEM_BYTES),
    )(order, chunk, slots)


def depth_order(tile_list, tile_slot, brick_rank):
    swap_count, brick_count = brick_rank.shape
    numbers = jnp.arange(brick_count, dtype=jnp.int32)
    placed = brick_rank[:, None, :] == numbers[None, :, None]
    order = jnp.sum(jnp.where(placed, numbers[None, None, :], 0), axis=2)
    found = tile_list[..., None] == jnp.arange(tile_slot.shape[0], dtype=jnp.int32)
    slots = jnp.sum(jnp.where(found, tile_slot, 0), axis=-1)
    slots = jnp.einsum(
        "srb,sbf->srf",
        placed.astype(jnp.float32),
        slots.reshape(swap_count, brick_count, -1).astype(jnp.float32),
        precision=lax.Precision.HIGHEST,
    )
    return order.reshape(-1), jnp.round(slots).reshape(1, -1)


def chunk_shards(samples, tile_list, tile_slot, brick_rank):
    group_count = lax.axis_size("grp")
    swap_count = lax.axis_size("swap")
    per_device, pixels = samples.shape[2], samples.shape[4]
    owned = tile_slot.shape[0] // group_count
    leaving = render_chunks(samples[0, 0], group_count, swap_count)
    arrived = lax.all_to_all(
        leaving.reshape(group_count * swap_count, 3, per_device, LANES),
        ("grp", "swap"),
        split_axis=0,
        concat_axis=0,
        tiled=True,
    )
    order, slots = depth_order(tile_list, tile_slot, brick_rank)
    arrived = arrived.reshape(leaving.shape)
    tiles = composite(order, arrived, slots, tile_slot.shape[0])
    image = lax.all_to_all(tiles, "grp", split_axis=0, concat_axis=0, tiled=True)
    red, green, opacity = (
        jnp.transpose(image[:, channel], (1, 0, 2)).reshape(owned, pixels // swap_count)
        for channel in range(3)
    )
    return jnp.stack([red, green, opacity - red, opacity], axis=1)[None]


def shards(samples, tile_list, tile_slot, brick_rank):
    device_count = lax.axis_size("grp") * lax.axis_size("swap")
    fragment_count = tile_list.shape[1] * tile_list.shape[2]
    if samples.shape[4] == device_count * LANES and fragment_count <= 1024:
        return chunk_shards(samples, tile_list, tile_slot, brick_rank)
    return general_shards(samples, tile_list, tile_slot, brick_rank)


def solution(mesh):
    return jax.shard_map(
        shards,
        mesh=mesh,
        in_specs=(P("swap", "grp", None, None, None), P(), P(), P()),
        out_specs=P("grp", None, None, "swap"),
        check_vma=False,
    )
```

```python
import functools
import jax
import jax.numpy as jnp
from jax import lax
from jax.experimental import pallas as pl
from jax.experimental.pallas import tpu as pltpu
from jax.sharding import PartitionSpec as P

BRICKS = 8


EXTINCTION = 0.024


def from_partner(array, axis, apart):
    return lax.ppermute(array, axis, [(i, i ^ 1 << apart) for i in range(lax.axis_size(axis))])


def render(values_in):
    depth_count = values_in.shape[1]
    shape = (values_in.shape[0], values_in.shape[2])
    before = jnp.zeros(shape, jnp.float32)
    red_sum = jnp.zeros(shape, jnp.float32)
    green_sum = jnp.zeros(shape, jnp.float32)
    blue_sum = jnp.zeros(shape, jnp.float32)
    for level in range(depth_count):
        values = values_in[:, level].astype(jnp.float32)
        extinction = EXTINCTION * values
        weight = jnp.exp(-before) * (1.0 - jnp.exp(-extinction))
        ratio = values / (1.0 + values)
        red_sum = red_sum + weight * ratio
        green_sum = green_sum + weight * 4.0 * ratio * (1.0 - ratio)
        blue_sum = blue_sum + weight * (1.0 - ratio)
        before = before + extinction
    return jnp.stack([red_sum, green_sum, blue_sum, before], axis=1)


def over_pair(front_part, back_part):
    colors = front_part[:, :3] + jnp.exp(-front_part[:, 3:4]) * back_part[:, :3]
    return jnp.concatenate([colors, front_part[:, 3:4] + back_part[:, 3:4]], axis=1)


def slot_tables(tiles_in, tile_slot, owned, per_brick, ranks_in):
    group_count, per_device = tiles_in.shape
    slot_ids = tile_slot[tiles_in]
    owners = slot_ids // owned
    tile_rows = slot_ids % owned
    position = jnp.arange(per_device, dtype=jnp.int32)
    same_owner = (owners[:, :, None] == owners[:, None, :]) & (
        position[None, None, :] < position[None, :, None]
    )
    places = jnp.sum(same_owner.astype(jnp.int32), axis=2)
    depth_keys = jnp.repeat(ranks_in.reshape(group_count, BRICKS), per_brick, axis=1)
    return (owners, tile_rows, places, depth_keys)


def arrivals(owners, tile_rows, places, depth_keys, device, capacity):
    slot_ids = jnp.arange(capacity, dtype=jnp.int32)
    matched = (
        (owners[:, None, :] == device) & (places[:, None, :] == slot_ids[None, :, None])
    ).astype(jnp.int32)
    rows_in = jnp.sum(matched * tile_rows[:, None, :], axis=2).reshape(-1)
    keys_in = jnp.sum(matched * depth_keys[:, None, :], axis=2).reshape(-1)
    valid_in = (jnp.sum(matched, axis=2) > 0).reshape(-1)
    return (rows_in, keys_in, valid_in)


def outgoing(fragments, owners_mine, places_mine, group_count, capacity):
    per_device = fragments.shape[0]
    target = owners_mine * capacity + places_mine
    slot_ids = jnp.arange(group_count * capacity, dtype=jnp.int32)
    matched = (target[None, :] == slot_ids[:, None]).astype(jnp.int32)
    numbers = jnp.arange(per_device, dtype=jnp.int32) + 1
    source = jnp.sum(matched * numbers[None, :], axis=1) - 1
    source = jnp.where(source < 0, per_device, source)
    padded = jnp.concatenate(
        [fragments, jnp.zeros((1,) + fragments.shape[1:], jnp.float32)], axis=0
    )
    return jnp.take(padded, source, axis=0)


def combine(pieces, rows_in, keys_in, valid_in, owned):
    optical = pieces[:, 3]
    both_valid = valid_in[:, None] & valid_in[None, :]
    in_front = (
        (rows_in[:, None] == rows_in[None, :]) & both_valid & (keys_in[None, :] < keys_in[:, None])
    ).astype(jnp.float32)
    prefix = jnp.dot(
        in_front, optical, precision=lax.Precision.HIGHEST, preferred_element_type=jnp.float32
    )
    shaded = pieces[:, :3] * jnp.exp(-prefix)[:, None]
    to_rows = (
        (jnp.arange(owned, dtype=jnp.int32)[:, None] == rows_in[None, :]) & valid_in[None, :]
    ).astype(jnp.float32)
    colors = jnp.einsum("of,fcp->ocp", to_rows, shaded, precision=lax.Precision.HIGHEST)
    summed = jnp.dot(
        to_rows, optical, precision=lax.Precision.HIGHEST, preferred_element_type=jnp.float32
    )
    return jnp.concatenate([colors, summed[:, None]], axis=1)


def leaving_of(fragments, owners_slab, places_slab, device, group_count, capacity):
    owners_mine = lax.dynamic_index_in_dim(owners_slab, device, 0, keepdims=False)
    places_mine = lax.dynamic_index_in_dim(places_slab, device, 0, keepdims=False)
    return outgoing(fragments, owners_mine, places_mine, group_count, capacity)


def general_shards(samples, tile_list, tile_slot, brick_rank):
    group_count = lax.axis_size("grp")
    swap_count = lax.axis_size("swap")
    device = lax.axis_index("grp")
    slab = lax.axis_index("swap")
    per_device = tile_list.shape[2]
    per_brick = per_device // BRICKS
    owned = tile_slot.shape[0] // group_count
    capacity = 2 * per_device // group_count
    pixels = samples.shape[4]
    block = pixels // swap_count
    fragments = render(samples[0, 0])
    tiles_slab = lax.dynamic_index_in_dim(tile_list, slab, 0, keepdims=False)
    ranks_slab = lax.dynamic_index_in_dim(brick_rank, slab, 0, keepdims=False)
    owners_slab, rows_slab, places_slab, keys_slab = slot_tables(
        tiles_slab, tile_slot, owned, per_brick, ranks_slab
    )
    leaving = leaving_of(fragments, owners_slab, places_slab, device, group_count, capacity)
    rows_in, keys_in, valid_in = arrivals(
        owners_slab, rows_slab, places_slab, keys_slab, device, capacity
    )
    arrived = lax.all_to_all(
        leaving.reshape(group_count, capacity, 4, pixels),
        "grp",
        split_axis=0,
        concat_axis=0,
        tiled=True,
    )
    partial_value = combine(
        arrived.reshape(-1, 4, arrived.shape[3]), rows_in, keys_in, valid_in, owned
    )
    levels = swap_count.bit_length() - 1
    partial_value = partial_value.reshape((owned, 4) + (2,) * levels + (block,))
    for level in range(levels):
        lower = partial_value[..., 0, :]
        upper = partial_value[..., 1, :]
        my_bit = jnp.right_shift(slab, level) % 2
        kept = jnp.where(my_bit == 1, upper, lower)
        given = jnp.where(my_bit == 1, lower, upper)
        received = from_partner(given, "swap", level)
        front_part = jnp.where(my_bit == 0, kept, received)
        back_part = jnp.where(my_bit == 0, received, kept)
        partial_value = over_pair(front_part, back_part)
    final_image = jnp.concatenate(
        [partial_value[:, :3], 1.0 - jnp.exp(-partial_value[:, 3:4])], axis=1
    )
    return final_image[None]


LANES = 128
VMEM_BYTES = 20 * 1024 * 1024


def level_order(fragments, depth_count):
    rows = fragments * depth_count
    to = lax.broadcasted_iota(jnp.int32, (rows, rows), 0)
    source = lax.broadcasted_iota(jnp.int32, (rows, rows), 1)
    wanted = (to % fragments) * depth_count + to // fragments
    return jnp.where(source == wanted, 1.0, 0.0).astype(jnp.bfloat16)


def render_levels(levels):
    before = through = held = held_twice = None
    for level in range(levels.shape[0]):
        values = levels[level]
        extinction = EXTINCTION * values
        before = extinction if before is None else before + extinction
        after = jnp.exp(-before)
        weight = (1.0 - after) if through is None else (through - after)
        through = after
        absent = 1.0 / (1.0 + values)
        once = weight * absent
        twice = once * absent
        held = once if held is None else held + once
        held_twice = twice if held_twice is None else held_twice + twice
    return (1.0 - through) - held, 4.0 * (held - held_twice), before


def render_kernel(groups, samples_ref, out_ref, held_ref, made_ref, in_sems, out_sems):
    group_count = out_ref.shape[0]
    _, depth_count, pixels = samples_ref.shape
    width = 8 * LANES
    arriving, leaving = [], []
    for at, (first, count) in enumerate(groups):
        rows = pl.ds(first, count)
        arriving.append(
            pltpu.make_async_copy(samples_ref.at[rows], held_ref.at[rows], in_sems.at[at])
        )
        place = (slice(None), slice(None), slice(None), rows)
        leaving.append(
            pltpu.make_async_copy(made_ref.at[place], out_ref.at[place], out_sems.at[at])
        )
    for copy in arriving:
        copy.start()
    for at, (first, count) in enumerate(groups):
        order = level_order(count, depth_count)
        arriving[at].wait()
        for start in range(0, pixels, width):
            levels = jnp.dot(
                order,
                held_ref[first : first + count, :, start : start + width].reshape(
                    count * depth_count, width
                ),
                preferred_element_type=jnp.float32,
            ).reshape(depth_count, count, width)
            for part in range(width // LANES):
                channels = render_levels(levels[:, :, part * LANES : (part + 1) * LANES])
                chunk = start // LANES + part
                for channel in range(3):
                    made_ref[
                        chunk % group_count, chunk // group_count, channel, first : first + count, :
                    ] = channels[channel]
        leaving[at].start()
    for copy in leaving:
        copy.wait()


def render_chunks(samples, group_count, swap_count):
    fragments = samples.shape[0]
    counts = [8] + [16] * (fragments // 16 - 1) + [8]
    groups = [(sum(counts[:at]), count) for at, count in enumerate(counts)]
    out_shape = (group_count, swap_count, 3, fragments, LANES)
    return pl.pallas_call(
        functools.partial(render_kernel, groups),
        in_specs=[pl.BlockSpec(memory_space=pltpu.HBM)],
        out_specs=pl.BlockSpec(memory_space=pltpu.HBM),
        out_shape=jax.ShapeDtypeStruct(out_shape, jnp.float32),
        scratch_shapes=[
            pltpu.VMEM(samples.shape, jnp.bfloat16),
            pltpu.VMEM(out_shape, jnp.float32),
            pltpu.SemaphoreType.DMA((len(groups),)),
            pltpu.SemaphoreType.DMA((len(groups),)),
        ],
        compiler_params=pltpu.CompilerParams(vmem_limit_bytes=3 * VMEM_BYTES),
    )(pltpu.with_memory_space_constraint(samples, pltpu.HBM))


def split(values):
    high = values.astype(jnp.bfloat16)
    low = (values - high.astype(jnp.float32)).astype(jnp.bfloat16)
    return jnp.concatenate([high, low], axis=1)


def masked_sum(mask, parts):
    both = jnp.dot(mask, parts, preferred_element_type=jnp.float32)
    width = parts.shape[1] // 2
    return both[:, :width] + both[:, width:]


def composite_kernel(per_device, rows_ref, chunk_ref, slots_ref, out_ref, sorted_ref):
    fragment_count = sorted_ref.shape[0]
    group_count, channels, _, lanes = out_ref.shape
    bricks = rows_ref.shape[0]
    per_brick = fragment_count // bricks
    for at in range(bricks):
        first = rows_ref[at]
        for channel in range(channels):
            source = pl.multiple_of(first + channel * per_device, per_brick)
            sorted_ref[
                at * per_brick : (at + 1) * per_brick, channel * lanes : (channel + 1) * lanes
            ] = chunk_ref[pl.ds(source, per_brick), :]
    block = min(2 * LANES, fragment_count)
    starts = range(0, fragment_count, block)
    row = lax.broadcasted_iota(jnp.int32, (block, block), 0) // per_brick
    column = lax.broadcasted_iota(jnp.int32, (block, block), 1) // per_brick
    nearer = column < row
    slot_count = group_count * out_ref.shape[2]
    slot_id = lax.broadcasted_iota(jnp.int32, (slot_count, block), 0).astype(jnp.float32)
    members, backs = [], []
    for start in starts:
        found = jnp.where(slots_ref[:, start : start + block] == slot_id, 1.0, 0.0)
        members.append(found.astype(jnp.bfloat16))
        backs.append(found.T.astype(jnp.bfloat16))
    opticals = [split(sorted_ref[start : start + block, 2 * lanes :]) for start in starts]
    added = [masked_sum(member, optical) for member, optical in zip(members, opticals)]
    fronts = []
    for member, back in zip(members, backs):
        same = jnp.dot(back, member, preferred_element_type=jnp.float32)
        fronts.append(jnp.where(nearer, same, 0.0).astype(jnp.bfloat16))
    depths = [added[0]]
    for value in added[1:]:
        depths.append(depths[-1] + value)
    throughs = []
    for at, (front, back, optical) in enumerate(zip(fronts, backs, opticals)):
        before = masked_sum(front, optical)
        if at > 0:
            before = before + masked_sum(back, split(depths[at - 1]))
        throughs.append(jnp.exp(-before))
    color = None
    for start, member, through in zip(starts, members, throughs):
        both = jnp.concatenate([through, through], axis=1)
        shaded = split(sorted_ref[start : start + block, : 2 * lanes] * both)
        shaded = masked_sum(member, shaded)
        color = shaded if color is None else color + shaded
    tiles = (group_count, out_ref.shape[2], lanes)
    out_ref[:, 0] = color[:, :lanes].reshape(tiles)
    out_ref[:, 1] = color[:, lanes:].reshape(tiles)
    out_ref[:, 2] = (1.0 - jnp.exp(-depths[-1])).reshape(tiles)


def composite(order, chunk, slots, slot_count):
    group_count, swap_count, channels, per_device, lanes = chunk.shape
    slabs = jnp.arange(swap_count, dtype=jnp.int32)[:, None]
    rows = ((order // BRICKS * swap_count + slabs) * channels) * per_device
    rows = rows + order % BRICKS * (per_device // BRICKS)
    vmem = pl.BlockSpec(memory_space=pltpu.VMEM)
    return pl.pallas_call(
        functools.partial(composite_kernel, per_device),
        in_specs=[pl.BlockSpec(memory_space=pltpu.SMEM), vmem, vmem],
        out_specs=vmem,
        out_shape=jax.ShapeDtypeStruct(
            (group_count, channels, slot_count // group_count, lanes), jnp.float32
        ),
        scratch_shapes=[pltpu.VMEM((slots.shape[1], channels * lanes), jnp.float32)],
        compiler_params=pltpu.CompilerParams(vmem_limit_bytes=VMEM_BYTES),
    )(rows.reshape(-1), chunk.reshape(-1, lanes), slots)


def depth_order(tile_list, tile_slot, brick_rank):
    swap_count, brick_count = brick_rank.shape
    numbers = jnp.arange(brick_count, dtype=jnp.int32)
    placed = brick_rank[:, None, :] == numbers[None, :, None]
    order = jnp.sum(jnp.where(placed, numbers[None, None, :], 0), axis=2)
    found = tile_list[..., None] == jnp.arange(tile_slot.shape[0], dtype=jnp.int32)
    slots = jnp.sum(jnp.where(found, tile_slot, 0), axis=-1)
    slots = jnp.einsum(
        "srb,sbf->srf",
        placed.astype(jnp.float32),
        slots.reshape(swap_count, brick_count, -1).astype(jnp.float32),
        precision=lax.Precision.HIGHEST,
    )
    return order, jnp.round(slots).reshape(1, -1)


def chunk_shards(samples, tile_list, tile_slot, brick_rank):
    group_count = lax.axis_size("grp")
    swap_count = lax.axis_size("swap")
    per_device, pixels = samples.shape[2], samples.shape[4]
    owned = tile_slot.shape[0] // group_count
    leaving = render_chunks(samples[0, 0], group_count, swap_count)
    arrived = lax.all_to_all(
        leaving.reshape(group_count * swap_count, 3, per_device, LANES),
        ("grp", "swap"),
        split_axis=0,
        concat_axis=0,
        tiled=True,
    )
    order, slots = depth_order(tile_list, tile_slot, brick_rank)
    arrived = arrived.reshape(leaving.shape)
    tiles = composite(order, arrived, slots, tile_slot.shape[0])
    image = lax.all_to_all(tiles, "grp", split_axis=0, concat_axis=0, tiled=True)
    red, green, opacity = (
        jnp.transpose(image[:, channel], (1, 0, 2)).reshape(owned, pixels // swap_count)
        for channel in range(3)
    )
    return jnp.stack([red, green, opacity - red, opacity], axis=1)[None]


def shards(samples, tile_list, tile_slot, brick_rank):
    device_count = lax.axis_size("grp") * lax.axis_size("swap")
    fragment_count = tile_list.shape[1] * tile_list.shape[2]
    if samples.shape[4] == device_count * LANES and fragment_count <= 1024:
        return chunk_shards(samples, tile_list, tile_slot, brick_rank)
    return general_shards(samples, tile_list, tile_slot, brick_rank)


def solution(mesh):
    return jax.shard_map(
        shards,
        mesh=mesh,
        in_specs=(P("swap", "grp", None, None, None), P(), P(), P()),
        out_specs=P("grp", None, None, "swap"),
        check_vma=False,
    )
```

```python
import functools
import jax
import jax.numpy as jnp
from jax import lax
from jax.experimental import pallas as pl
from jax.experimental.pallas import tpu as pltpu
from jax.sharding import PartitionSpec as P

BRICKS = 8


EXTINCTION = 0.024


def from_partner(array, axis, apart):
    return lax.ppermute(array, axis, [(i, i ^ 1 << apart) for i in range(lax.axis_size(axis))])


def render(values_in):
    depth_count = values_in.shape[1]
    shape = (values_in.shape[0], values_in.shape[2])
    before = jnp.zeros(shape, jnp.float32)
    red_sum = jnp.zeros(shape, jnp.float32)
    green_sum = jnp.zeros(shape, jnp.float32)
    blue_sum = jnp.zeros(shape, jnp.float32)
    for level in range(depth_count):
        values = values_in[:, level].astype(jnp.float32)
        extinction = EXTINCTION * values
        weight = jnp.exp(-before) * (1.0 - jnp.exp(-extinction))
        ratio = values / (1.0 + values)
        red_sum = red_sum + weight * ratio
        green_sum = green_sum + weight * 4.0 * ratio * (1.0 - ratio)
        blue_sum = blue_sum + weight * (1.0 - ratio)
        before = before + extinction
    return jnp.stack([red_sum, green_sum, blue_sum, before], axis=1)


def over_pair(front_part, back_part):
    colors = front_part[:, :3] + jnp.exp(-front_part[:, 3:4]) * back_part[:, :3]
    return jnp.concatenate([colors, front_part[:, 3:4] + back_part[:, 3:4]], axis=1)


def slot_tables(tiles_in, tile_slot, owned, per_brick, ranks_in):
    group_count, per_device = tiles_in.shape
    slot_ids = tile_slot[tiles_in]
    owners = slot_ids // owned
    tile_rows = slot_ids % owned
    position = jnp.arange(per_device, dtype=jnp.int32)
    same_owner = (owners[:, :, None] == owners[:, None, :]) & (
        position[None, None, :] < position[None, :, None]
    )
    places = jnp.sum(same_owner.astype(jnp.int32), axis=2)
    depth_keys = jnp.repeat(ranks_in.reshape(group_count, BRICKS), per_brick, axis=1)
    return (owners, tile_rows, places, depth_keys)


def arrivals(owners, tile_rows, places, depth_keys, device, capacity):
    slot_ids = jnp.arange(capacity, dtype=jnp.int32)
    matched = (
        (owners[:, None, :] == device) & (places[:, None, :] == slot_ids[None, :, None])
    ).astype(jnp.int32)
    rows_in = jnp.sum(matched * tile_rows[:, None, :], axis=2).reshape(-1)
    keys_in = jnp.sum(matched * depth_keys[:, None, :], axis=2).reshape(-1)
    valid_in = (jnp.sum(matched, axis=2) > 0).reshape(-1)
    return (rows_in, keys_in, valid_in)


def outgoing(fragments, owners_mine, places_mine, group_count, capacity):
    per_device = fragments.shape[0]
    target = owners_mine * capacity + places_mine
    slot_ids = jnp.arange(group_count * capacity, dtype=jnp.int32)
    matched = (target[None, :] == slot_ids[:, None]).astype(jnp.int32)
    numbers = jnp.arange(per_device, dtype=jnp.int32) + 1
    source = jnp.sum(matched * numbers[None, :], axis=1) - 1
    source = jnp.where(source < 0, per_device, source)
    padded = jnp.concatenate(
        [fragments, jnp.zeros((1,) + fragments.shape[1:], jnp.float32)], axis=0
    )
    return jnp.take(padded, source, axis=0)


def combine(pieces, rows_in, keys_in, valid_in, owned):
    optical = pieces[:, 3]
    both_valid = valid_in[:, None] & valid_in[None, :]
    in_front = (
        (rows_in[:, None] == rows_in[None, :]) & both_valid & (keys_in[None, :] < keys_in[:, None])
    ).astype(jnp.float32)
    prefix = jnp.dot(
        in_front, optical, precision=lax.Precision.HIGHEST, preferred_element_type=jnp.float32
    )
    shaded = pieces[:, :3] * jnp.exp(-prefix)[:, None]
    to_rows = (
        (jnp.arange(owned, dtype=jnp.int32)[:, None] == rows_in[None, :]) & valid_in[None, :]
    ).astype(jnp.float32)
    colors = jnp.einsum("of,fcp->ocp", to_rows, shaded, precision=lax.Precision.HIGHEST)
    summed = jnp.dot(
        to_rows, optical, precision=lax.Precision.HIGHEST, preferred_element_type=jnp.float32
    )
    return jnp.concatenate([colors, summed[:, None]], axis=1)


def leaving_of(fragments, owners_slab, places_slab, device, group_count, capacity):
    owners_mine = lax.dynamic_index_in_dim(owners_slab, device, 0, keepdims=False)
    places_mine = lax.dynamic_index_in_dim(places_slab, device, 0, keepdims=False)
    return outgoing(fragments, owners_mine, places_mine, group_count, capacity)


def general_shards(samples, tile_list, tile_slot, brick_rank):
    group_count = lax.axis_size("grp")
    swap_count = lax.axis_size("swap")
    device = lax.axis_index("grp")
    slab = lax.axis_index("swap")
    per_device = tile_list.shape[2]
    per_brick = per_device // BRICKS
    owned = tile_slot.shape[0] // group_count
    capacity = 2 * per_device // group_count
    pixels = samples.shape[4]
    block = pixels // swap_count
    fragments = render(samples[0, 0])
    tiles_slab = lax.dynamic_index_in_dim(tile_list, slab, 0, keepdims=False)
    ranks_slab = lax.dynamic_index_in_dim(brick_rank, slab, 0, keepdims=False)
    owners_slab, rows_slab, places_slab, keys_slab = slot_tables(
        tiles_slab, tile_slot, owned, per_brick, ranks_slab
    )
    leaving = leaving_of(fragments, owners_slab, places_slab, device, group_count, capacity)
    rows_in, keys_in, valid_in = arrivals(
        owners_slab, rows_slab, places_slab, keys_slab, device, capacity
    )
    arrived = lax.all_to_all(
        leaving.reshape(group_count, capacity, 4, pixels),
        "grp",
        split_axis=0,
        concat_axis=0,
        tiled=True,
    )
    partial_value = combine(
        arrived.reshape(-1, 4, arrived.shape[3]), rows_in, keys_in, valid_in, owned
    )
    levels = swap_count.bit_length() - 1
    partial_value = partial_value.reshape((owned, 4) + (2,) * levels + (block,))
    for level in range(levels):
        lower = partial_value[..., 0, :]
        upper = partial_value[..., 1, :]
        my_bit = jnp.right_shift(slab, level) % 2
        kept = jnp.where(my_bit == 1, upper, lower)
        given = jnp.where(my_bit == 1, lower, upper)
        received = from_partner(given, "swap", level)
        front_part = jnp.where(my_bit == 0, kept, received)
        back_part = jnp.where(my_bit == 0, received, kept)
        partial_value = over_pair(front_part, back_part)
    final_image = jnp.concatenate(
        [partial_value[:, :3], 1.0 - jnp.exp(-partial_value[:, 3:4])], axis=1
    )
    return final_image[None]


LANES = 128
VMEM_BYTES = 20 * 1024 * 1024


def level_order(fragments, depth_count):
    rows = fragments * depth_count
    to = lax.broadcasted_iota(jnp.int32, (rows, rows), 0)
    source = lax.broadcasted_iota(jnp.int32, (rows, rows), 1)
    wanted = (to % fragments) * depth_count + to // fragments
    return jnp.where(source == wanted, 1.0, 0.0).astype(jnp.bfloat16)


def render_levels(levels):
    before = through = held = held_twice = None
    for level in range(levels.shape[0]):
        values = levels[level]
        extinction = EXTINCTION * values
        before = extinction if before is None else before + extinction
        after = jnp.exp(-before)
        weight = (1.0 - after) if through is None else (through - after)
        through = after
        absent = 1.0 / (1.0 + values)
        once = weight * absent
        twice = once * absent
        held = once if held is None else held + once
        held_twice = twice if held_twice is None else held_twice + twice
    return (1.0 - through) - held, 4.0 * (held - held_twice), before


def render_pair(device, slab, samples_ref, order, offset):
    fragments, depth_count, pixels = samples_ref.shape
    half = pixels // 2
    picked = []
    for flip in range(2):
        first = jnp.bitwise_xor(slab, flip) * half + jnp.bitwise_xor(device, offset) * LANES
        picked.append(samples_ref[:, :, pl.ds(pl.multiple_of(first, LANES), LANES)])
    levels = jnp.dot(
        order,
        jnp.concatenate(picked, axis=2).reshape(fragments * depth_count, 2 * LANES),
        preferred_element_type=jnp.float32,
    ).reshape(depth_count, fragments, 2 * LANES)
    channels = render_levels(levels)
    return [[value[:, at * LANES : (at + 1) * LANES] for value in channels] for at in range(2)]


def pair_kernel(offsets, singles, numbers_ref, samples_ref, *out_refs):
    order = level_order(*samples_ref.shape[:2])
    targets = [[ref.at[0], ref.at[1]] for ref in out_refs[: len(offsets)]]
    rest = out_refs[len(offsets) :]
    targets += [rest[at : at + 2] for at in range(0, len(rest), 2)]
    for target, offset in zip(targets, offsets + singles):
        pair = render_pair(numbers_ref[0], numbers_ref[1], samples_ref, order, offset)
        for flip in range(2):
            for channel in range(3):
                target[flip][channel] = pair[flip][channel]


def near_kernel(near, numbers_ref, samples_ref, *refs):
    out_ref = refs[-1]
    order = level_order(*samples_ref.shape[:2])
    device, slab = numbers_ref[0], numbers_ref[1]
    for offset in range(near):
        pair = render_pair(device, slab, samples_ref, order, offset)
        for flip in range(2):
            entry = lax.rem(jnp.bitwise_xor(device, offset), near) * 2 + jnp.bitwise_xor(slab, flip)
            for channel in range(3):
                out_ref[entry, channel] = pair[flip][channel]


def on_device(kernel, out_shapes, numbers, *arrays):
    vmem = pl.BlockSpec(memory_space=pltpu.VMEM)
    return pl.pallas_call(
        kernel,
        in_specs=[pl.BlockSpec(memory_space=pltpu.SMEM)] + [vmem] * len(arrays),
        out_specs=[vmem] * len(out_shapes),
        out_shape=[jax.ShapeDtypeStruct(shape, jnp.float32) for shape in out_shapes],
        compiler_params=pltpu.CompilerParams(vmem_limit_bytes=VMEM_BYTES),
    )(numbers, *arrays)


def split(values):
    high = values.astype(jnp.bfloat16)
    low = (values - high.astype(jnp.float32)).astype(jnp.bfloat16)
    return jnp.concatenate([high, low], axis=1)


def masked_sum(mask, parts):
    both = jnp.dot(mask, parts, preferred_element_type=jnp.float32)
    width = parts.shape[1] // 2
    return both[:, :width] + both[:, width:]


def slots_kernel(slots_ref, *refs):
    refs[-1][...] = jnp.round(slots_ref[...])


def composite_kernel(picks, late, places_ref, slots_ref, *refs):
    count = 1 + max(array for array, _ in picks)
    chunk_refs, (out_ref, sorted_ref, held_ref, sems) = refs[:count], refs[count:]
    chunks, copies = [], []
    for array, index in picks:
        chunk = chunk_refs[array] if index is None else chunk_refs[array].at[index]
        if array in late:
            chunks.append((chunk, None))
        else:
            slot = len(copies)
            copies.append(pltpu.make_async_copy(chunk, held_ref.at[slot], sems.at[slot]))
            copies[-1].start()
            chunks.append((held_ref.at[slot], copies[-1]))
    channels, per_device, lanes = held_ref.shape[1:]
    fragment_count = sorted_ref.shape[0]
    group_count = out_ref.shape[0]
    per_brick = per_device // BRICKS
    for at in sorted(range(len(picks)), key=lambda at: chunks[at][1] is not None):
        chunk, copy = chunks[at]
        if copy is not None:
            copy.wait()
        for brick in range(BRICKS):
            place = pl.multiple_of(places_ref[at * BRICKS + brick], per_brick)
            rows = slice(brick * per_brick, (brick + 1) * per_brick)
            for channel in range(channels):
                sorted_ref[
                    pl.ds(place, per_brick), channel * lanes : (channel + 1) * lanes
                ] = chunk[channel, rows, :]
    block = min(2 * LANES, fragment_count)
    starts = range(0, fragment_count, block)
    row = lax.broadcasted_iota(jnp.int32, (block, block), 0) // per_brick
    column = lax.broadcasted_iota(jnp.int32, (block, block), 1) // per_brick
    nearer = column < row
    slot_count = group_count * out_ref.shape[2]
    slot_id = lax.broadcasted_iota(jnp.int32, (slot_count, block), 0).astype(jnp.float32)
    members, backs = [], []
    for start in starts:
        found = jnp.where(slots_ref[:, start : start + block] == slot_id, 1.0, 0.0)
        members.append(found.astype(jnp.bfloat16))
        backs.append(found.T.astype(jnp.bfloat16))
    opticals = [split(sorted_ref[start : start + block, 2 * lanes :]) for start in starts]
    added = [masked_sum(member, optical) for member, optical in zip(members, opticals)]
    fronts = []
    for member, back in zip(members, backs):
        same = jnp.dot(back, member, preferred_element_type=jnp.float32)
        fronts.append(jnp.where(nearer, same, 0.0).astype(jnp.bfloat16))
    depths = [added[0]]
    for value in added[1:]:
        depths.append(depths[-1] + value)
    throughs = []
    for at, (front, back, optical) in enumerate(zip(fronts, backs, opticals)):
        before = masked_sum(front, optical)
        if at > 0:
            before = before + masked_sum(back, split(depths[at - 1]))
        throughs.append(jnp.exp(-before))
    color = None
    for start, member, through in zip(starts, members, throughs):
        both = jnp.concatenate([through, through], axis=1)
        shaded = split(sorted_ref[start : start + block, : 2 * lanes] * both)
        shaded = masked_sum(member, shaded)
        color = shaded if color is None else color + shaded
    tiles = (group_count, out_ref.shape[2], lanes)
    out_ref[:, 0] = color[:, :lanes].reshape(tiles)
    out_ref[:, 1] = color[:, lanes:].reshape(tiles)
    out_ref[:, 2] = (1.0 - jnp.exp(-depths[-1])).reshape(tiles)


def composite(places, arrays, picks, late, slots, slot_count, group_count):
    smem, vmem = pl.BlockSpec(memory_space=pltpu.SMEM), pl.BlockSpec(memory_space=pltpu.VMEM)
    hbm = pl.BlockSpec(memory_space=pltpu.HBM)
    held = (sum(array not in late for array, _ in picks),) + arrays[0].shape[-3:]
    specs = [vmem if at in late else hbm for at in range(len(arrays))]
    arrays = [
        array if at in late else pltpu.with_memory_space_constraint(array, pltpu.HBM)
        for at, array in enumerate(arrays)
    ]
    return pl.pallas_call(
        functools.partial(composite_kernel, picks, late),
        in_specs=[smem, vmem] + specs,
        out_specs=vmem,
        out_shape=jax.ShapeDtypeStruct(
            (group_count, 3, slot_count // group_count, LANES), jnp.float32
        ),
        scratch_shapes=[
            pltpu.VMEM((slots.shape[1], 3 * LANES), jnp.float32),
            pltpu.VMEM(held, jnp.float32),
            pltpu.SemaphoreType.DMA(held[:1]),
        ],
        compiler_params=pltpu.CompilerParams(vmem_limit_bytes=VMEM_BYTES),
    )(places, slots, *arrays)


def depth_slots(tile_list, tile_slot, brick_rank, after):
    swap_count, brick_count = brick_rank.shape
    numbers = jnp.arange(brick_count, dtype=jnp.int32)
    placed = brick_rank[:, None, :] == numbers[None, :, None]
    found = tile_list[..., None] == jnp.arange(tile_slot.shape[0], dtype=jnp.int32)
    slots = jnp.sum(jnp.where(found, tile_slot, 0), axis=-1)
    slots = jnp.einsum(
        "srb,sbf->srf",
        placed.astype(jnp.float32),
        slots.reshape(swap_count, brick_count, -1).astype(jnp.float32),
        precision=lax.Precision.HIGHEST,
    ).reshape(1, -1)
    vmem = pl.BlockSpec(memory_space=pltpu.VMEM)
    return pl.pallas_call(
        slots_kernel,
        in_specs=[vmem] + [pl.BlockSpec(memory_space=pl.ANY)] * len(after),
        out_specs=vmem,
        out_shape=jax.ShapeDtypeStruct(slots.shape, jnp.float32),
        compiler_params=pltpu.CompilerParams(vmem_limit_bytes=VMEM_BYTES),
        cost_estimate=pl.CostEstimate(flops=30000000000, bytes_accessed=0, transcendentals=0),
    )(slots, *after)


def chunk_shards(samples, tile_list, tile_slot, brick_rank):
    group_count = lax.axis_size("grp")
    swap_count = lax.axis_size("swap")
    device = lax.axis_index("grp").astype(jnp.int32)
    slab = lax.axis_index("swap").astype(jnp.int32)
    per_device, pixels = samples.shape[2], samples.shape[4]
    slot_count = tile_slot.shape[0]
    owned = slot_count // group_count
    numbers = jnp.stack([device, slab])
    mine = samples[0, 0]
    near = group_count // 2
    chunk = (3, per_device, LANES)

    def send(array, offset, flip):
        pairs = [
            (g * swap_count + s, (g ^ offset) * swap_count + (s ^ flip))
            for g in range(group_count)
            for s in range(swap_count)
        ]
        return lax.ppermute(array, ("grp", "swap"), pairs)

    relayed, direct = list(range(near, group_count - 4)), list(range(group_count - 4, group_count))
    leaving = on_device(
        functools.partial(pair_kernel, relayed[:2], []), [(2,) + chunk] * 2, numbers, mine
    )
    leaving += on_device(
        functools.partial(pair_kernel, relayed[2:], direct),
        [(2,) + chunk] * len(relayed[2:]) + [chunk] * (2 * len(direct)),
        numbers,
        mine,
    )
    (near_chunks,) = on_device(
        functools.partial(near_kernel, near), [(near * swap_count,) + chunk], numbers, mine
    )
    arrays, picks, sources = [], [], []

    def keep(array, entries):
        for index, source in entries:
            picks.append((len(arrays), index))
            sources.append(source)
        arrays.append(array)

    passing = []
    for offset, array in zip(relayed, leaving):
        got = send(array, offset, 0)
        keep(got, [(0, (offset, 0))])
        passing.append(got)
    singles = [(offset, flip) for offset in direct for flip in range(2)]
    for partner, array in zip(singles, leaving[len(relayed) :]):
        keep(send(array, *partner), [(None, partner)])
    late = set(range(len(relayed) + 1, len(arrays) + 1))
    for first, last in ((0, 4),):
        group = jnp.stack([got[1] for got in passing[first:last]])
        keep(
            send(group, 0, 1),
            [(at, (offset, 1)) for at, offset in enumerate(relayed[first:last])],
        )
    late.add(len(arrays))
    slots = depth_slots(tile_list, tile_slot, brick_rank, arrays)
    members = near * swap_count
    near_chunks = lax.all_to_all(
        near_chunks,
        ("grp", "swap"),
        split_axis=0,
        concat_axis=0,
        tiled=True,
        axis_index_groups=[list(range(members)), list(range(members, 2 * members))],
    )
    picks = [(0, at) for at in range(members)] + [(array + 1, index) for array, index in picks]
    arrays = [near_chunks] + arrays
    offsets = jnp.array([offset for offset, _ in sources], jnp.int32)
    flips = jnp.array([flip for _, flip in sources], jnp.int32)
    source = jnp.bitwise_xor(slab, flips) * group_count + jnp.bitwise_xor(device, offsets)
    entries = jnp.arange(members, dtype=jnp.int32)
    near_source = entries % swap_count * group_count + device // near * near + entries // swap_count
    source = jnp.concatenate([near_source, source])
    ranks = brick_rank.reshape(swap_count * group_count, BRICKS)
    ranks = ranks + jnp.repeat(jnp.arange(swap_count), group_count)[:, None] * brick_rank.shape[1]
    ids = jnp.arange(swap_count * group_count, dtype=jnp.int32)
    places = jnp.sum(jnp.where((source[:, None] == ids)[..., None], ranks[None], 0), axis=1)
    places = places.reshape(-1) * (per_device // BRICKS)
    tiles = composite(places, arrays, picks, late, slots, slot_count, group_count)
    image = lax.all_to_all(tiles, "grp", split_axis=0, concat_axis=0, tiled=True)
    red, green, opacity = (
        jnp.transpose(image[:, channel], (1, 0, 2)).reshape(owned, pixels // swap_count)
        for channel in range(3)
    )
    return jnp.stack([red, green, opacity - red, opacity], axis=1)[None]


def shards(samples, tile_list, tile_slot, brick_rank):
    device_count = lax.axis_size("grp") * lax.axis_size("swap")
    fragment_count = tile_list.shape[1] * tile_list.shape[2]
    if samples.shape[4] == device_count * LANES and fragment_count <= 1024:
        return chunk_shards(samples, tile_list, tile_slot, brick_rank)
    return general_shards(samples, tile_list, tile_slot, brick_rank)


def solution(mesh):
    return jax.shard_map(
        shards,
        mesh=mesh,
        in_specs=(P("swap", "grp", None, None, None), P(), P(), P()),
        out_specs=P("grp", None, None, "swap"),
        check_vma=False,
    )
```

```python
import functools
import jax
import jax.numpy as jnp
from jax import lax
from jax.experimental import pallas as pl
from jax.experimental.pallas import tpu as pltpu
from jax.sharding import PartitionSpec as P

BRICKS = 8


EXTINCTION = 0.024


def from_partner(array, axis, apart):
    return lax.ppermute(array, axis, [(i, i ^ 1 << apart) for i in range(lax.axis_size(axis))])


def render(values_in):
    depth_count = values_in.shape[1]
    shape = (values_in.shape[0], values_in.shape[2])
    before = jnp.zeros(shape, jnp.float32)
    red_sum = jnp.zeros(shape, jnp.float32)
    green_sum = jnp.zeros(shape, jnp.float32)
    blue_sum = jnp.zeros(shape, jnp.float32)
    for level in range(depth_count):
        values = values_in[:, level].astype(jnp.float32)
        extinction = EXTINCTION * values
        weight = jnp.exp(-before) * (1.0 - jnp.exp(-extinction))
        ratio = values / (1.0 + values)
        red_sum = red_sum + weight * ratio
        green_sum = green_sum + weight * 4.0 * ratio * (1.0 - ratio)
        blue_sum = blue_sum + weight * (1.0 - ratio)
        before = before + extinction
    return jnp.stack([red_sum, green_sum, blue_sum, before], axis=1)


def over_pair(front_part, back_part):
    colors = front_part[:, :3] + jnp.exp(-front_part[:, 3:4]) * back_part[:, :3]
    return jnp.concatenate([colors, front_part[:, 3:4] + back_part[:, 3:4]], axis=1)


def slot_tables(tiles_in, tile_slot, owned, per_brick, ranks_in):
    group_count, per_device = tiles_in.shape
    slot_ids = tile_slot[tiles_in]
    owners = slot_ids // owned
    tile_rows = slot_ids % owned
    position = jnp.arange(per_device, dtype=jnp.int32)
    same_owner = (owners[:, :, None] == owners[:, None, :]) & (
        position[None, None, :] < position[None, :, None]
    )
    places = jnp.sum(same_owner.astype(jnp.int32), axis=2)
    depth_keys = jnp.repeat(ranks_in.reshape(group_count, BRICKS), per_brick, axis=1)
    return (owners, tile_rows, places, depth_keys)


def arrivals(owners, tile_rows, places, depth_keys, device, capacity):
    slot_ids = jnp.arange(capacity, dtype=jnp.int32)
    matched = (
        (owners[:, None, :] == device) & (places[:, None, :] == slot_ids[None, :, None])
    ).astype(jnp.int32)
    rows_in = jnp.sum(matched * tile_rows[:, None, :], axis=2).reshape(-1)
    keys_in = jnp.sum(matched * depth_keys[:, None, :], axis=2).reshape(-1)
    valid_in = (jnp.sum(matched, axis=2) > 0).reshape(-1)
    return (rows_in, keys_in, valid_in)


def outgoing(fragments, owners_mine, places_mine, group_count, capacity):
    per_device = fragments.shape[0]
    target = owners_mine * capacity + places_mine
    slot_ids = jnp.arange(group_count * capacity, dtype=jnp.int32)
    matched = (target[None, :] == slot_ids[:, None]).astype(jnp.int32)
    numbers = jnp.arange(per_device, dtype=jnp.int32) + 1
    source = jnp.sum(matched * numbers[None, :], axis=1) - 1
    source = jnp.where(source < 0, per_device, source)
    padded = jnp.concatenate(
        [fragments, jnp.zeros((1,) + fragments.shape[1:], jnp.float32)], axis=0
    )
    return jnp.take(padded, source, axis=0)


def combine(pieces, rows_in, keys_in, valid_in, owned):
    optical = pieces[:, 3]
    both_valid = valid_in[:, None] & valid_in[None, :]
    in_front = (
        (rows_in[:, None] == rows_in[None, :]) & both_valid & (keys_in[None, :] < keys_in[:, None])
    ).astype(jnp.float32)
    prefix = jnp.dot(
        in_front, optical, precision=lax.Precision.HIGHEST, preferred_element_type=jnp.float32
    )
    shaded = pieces[:, :3] * jnp.exp(-prefix)[:, None]
    to_rows = (
        (jnp.arange(owned, dtype=jnp.int32)[:, None] == rows_in[None, :]) & valid_in[None, :]
    ).astype(jnp.float32)
    colors = jnp.einsum("of,fcp->ocp", to_rows, shaded, precision=lax.Precision.HIGHEST)
    summed = jnp.dot(
        to_rows, optical, precision=lax.Precision.HIGHEST, preferred_element_type=jnp.float32
    )
    return jnp.concatenate([colors, summed[:, None]], axis=1)


def leaving_of(fragments, owners_slab, places_slab, device, group_count, capacity):
    owners_mine = lax.dynamic_index_in_dim(owners_slab, device, 0, keepdims=False)
    places_mine = lax.dynamic_index_in_dim(places_slab, device, 0, keepdims=False)
    return outgoing(fragments, owners_mine, places_mine, group_count, capacity)


def general_shards(samples, tile_list, tile_slot, brick_rank):
    group_count = lax.axis_size("grp")
    swap_count = lax.axis_size("swap")
    device = lax.axis_index("grp")
    slab = lax.axis_index("swap")
    per_device = tile_list.shape[2]
    per_brick = per_device // BRICKS
    owned = tile_slot.shape[0] // group_count
    capacity = 2 * per_device // group_count
    pixels = samples.shape[4]
    block = pixels // swap_count
    fragments = render(samples[0, 0])
    tiles_slab = lax.dynamic_index_in_dim(tile_list, slab, 0, keepdims=False)
    ranks_slab = lax.dynamic_index_in_dim(brick_rank, slab, 0, keepdims=False)
    owners_slab, rows_slab, places_slab, keys_slab = slot_tables(
        tiles_slab, tile_slot, owned, per_brick, ranks_slab
    )
    leaving = leaving_of(fragments, owners_slab, places_slab, device, group_count, capacity)
    rows_in, keys_in, valid_in = arrivals(
        owners_slab, rows_slab, places_slab, keys_slab, device, capacity
    )
    arrived = lax.all_to_all(
        leaving.reshape(group_count, capacity, 4, pixels),
        "grp",
        split_axis=0,
        concat_axis=0,
        tiled=True,
    )
    partial_value = combine(
        arrived.reshape(-1, 4, arrived.shape[3]), rows_in, keys_in, valid_in, owned
    )
    levels = swap_count.bit_length() - 1
    partial_value = partial_value.reshape((owned, 4) + (2,) * levels + (block,))
    for level in range(levels):
        lower = partial_value[..., 0, :]
        upper = partial_value[..., 1, :]
        my_bit = jnp.right_shift(slab, level) % 2
        kept = jnp.where(my_bit == 1, upper, lower)
        given = jnp.where(my_bit == 1, lower, upper)
        received = from_partner(given, "swap", level)
        front_part = jnp.where(my_bit == 0, kept, received)
        back_part = jnp.where(my_bit == 0, received, kept)
        partial_value = over_pair(front_part, back_part)
    final_image = jnp.concatenate(
        [partial_value[:, :3], 1.0 - jnp.exp(-partial_value[:, 3:4])], axis=1
    )
    return final_image[None]


LANES = 128
VMEM_BYTES = 16 * 1024 * 1024


def level_order(fragments, depth_count):
    rows = fragments * depth_count
    to = lax.broadcasted_iota(jnp.int32, (rows, rows), 0)
    source = lax.broadcasted_iota(jnp.int32, (rows, rows), 1)
    wanted = (to % fragments) * depth_count + to // fragments
    return jnp.where(source == wanted, 1.0, 0.0).astype(jnp.bfloat16)


def render_levels(levels):
    before = through = held = held_twice = None
    for level in range(levels.shape[0]):
        values = levels[level]
        extinction = EXTINCTION * values
        before = extinction if before is None else before + extinction
        after = jnp.exp(-before)
        weight = (1.0 - after) if through is None else (through - after)
        through = after
        absent = 1.0 / (1.0 + values)
        once = weight * absent
        twice = once * absent
        held = once if held is None else held + once
        held_twice = twice if held_twice is None else held_twice + twice
    return (1.0 - through) - held, 4.0 * (held - held_twice), before


def render_pair(device, slab, samples_ref, order, offset):
    fragments, depth_count, pixels = samples_ref.shape
    half = pixels // 2
    picked = []
    for flip in range(2):
        first = jnp.bitwise_xor(slab, flip) * half + jnp.bitwise_xor(device, offset) * LANES
        picked.append(samples_ref[:, :, pl.ds(pl.multiple_of(first, LANES), LANES)])
    levels = jnp.dot(
        order,
        jnp.concatenate(picked, axis=2).reshape(fragments * depth_count, 2 * LANES),
        preferred_element_type=jnp.float32,
    ).reshape(depth_count, fragments, 2 * LANES)
    channels = render_levels(levels)
    return [[value[:, at * LANES : (at + 1) * LANES] for value in channels] for at in range(2)]


def pair_kernel(offsets, singles, numbers_ref, samples_ref, *out_refs):
    order = level_order(*samples_ref.shape[:2])
    targets = [[ref.at[0], ref.at[1]] for ref in out_refs[: len(offsets)]]
    rest = out_refs[len(offsets) :]
    targets += [rest[at : at + 2] for at in range(0, len(rest), 2)]
    for target, offset in zip(targets, offsets + singles):
        pair = render_pair(numbers_ref[0], numbers_ref[1], samples_ref, order, offset)
        for flip in range(2):
            for channel in range(3):
                target[flip][channel] = pair[flip][channel]


def near_kernel(near, numbers_ref, samples_ref, *refs):
    out_ref = refs[-1]
    order = level_order(*samples_ref.shape[:2])
    device, slab = numbers_ref[0], numbers_ref[1]
    for offset in range(near):
        pair = render_pair(device, slab, samples_ref, order, offset)
        for flip in range(2):
            entry = lax.rem(jnp.bitwise_xor(device, offset), near) * 2 + jnp.bitwise_xor(slab, flip)
            for channel in range(3):
                out_ref[entry, channel] = pair[flip][channel]


def on_device(kernel, out_shapes, numbers, *arrays):
    vmem = pl.BlockSpec(memory_space=pltpu.VMEM)
    return pl.pallas_call(
        kernel,
        in_specs=[pl.BlockSpec(memory_space=pltpu.SMEM)] + [vmem] * len(arrays),
        out_specs=[vmem] * len(out_shapes),
        out_shape=[jax.ShapeDtypeStruct(shape, jnp.float32) for shape in out_shapes],
        compiler_params=pltpu.CompilerParams(vmem_limit_bytes=VMEM_BYTES // 2),
    )(numbers, *arrays)


def split(values):
    high = values.astype(jnp.bfloat16)
    low = (values - high.astype(jnp.float32)).astype(jnp.bfloat16)
    return jnp.concatenate([high, low], axis=1)


def masked_sum(mask, parts):
    both = jnp.dot(mask, parts, preferred_element_type=jnp.float32)
    width = parts.shape[1] // 2
    return both[:, :width] + both[:, width:]


def slots_kernel(slots_ref, *refs):
    refs[-1][...] = jnp.round(slots_ref[...])


def composite_kernel(picks, late, places_ref, slots_ref, *refs):
    count = 1 + max(array for array, _ in picks)
    chunk_refs, (out_ref, sorted_ref, held_ref, sems) = refs[:count], refs[count:]
    chunks, copies = [], []
    for array, index in picks:
        chunk = chunk_refs[array] if index is None else chunk_refs[array].at[index]
        if array in late:
            chunks.append((chunk, None))
        else:
            slot = len(copies)
            copies.append(pltpu.make_async_copy(chunk, held_ref.at[slot], sems.at[slot]))
            copies[-1].start()
            chunks.append((held_ref.at[slot], copies[-1]))
    channels, per_device, lanes = held_ref.shape[1:]
    fragment_count = sorted_ref.shape[0]
    group_count = out_ref.shape[0]
    per_brick = per_device // BRICKS
    for at in sorted(range(len(picks)), key=lambda at: chunks[at][1] is not None):
        chunk, copy = chunks[at]
        if copy is not None:
            copy.wait()
        for brick in range(BRICKS):
            place = pl.multiple_of(places_ref[at * BRICKS + brick], per_brick)
            rows = slice(brick * per_brick, (brick + 1) * per_brick)
            for channel in range(channels):
                sorted_ref[
                    pl.ds(place, per_brick), channel * lanes : (channel + 1) * lanes
                ] = chunk[channel, rows, :]
    block = min(2 * LANES, fragment_count)
    starts = range(0, fragment_count, block)
    row = lax.broadcasted_iota(jnp.int32, (block, block), 0) // per_brick
    column = lax.broadcasted_iota(jnp.int32, (block, block), 1) // per_brick
    nearer = column < row
    slot_count = group_count * out_ref.shape[2]
    slot_id = lax.broadcasted_iota(jnp.int32, (slot_count, block), 0).astype(jnp.float32)
    members, backs = [], []
    for start in starts:
        found = jnp.where(slots_ref[:, start : start + block] == slot_id, 1.0, 0.0)
        members.append(found.astype(jnp.bfloat16))
        backs.append(found.T.astype(jnp.bfloat16))
    opticals = [split(sorted_ref[start : start + block, 2 * lanes :]) for start in starts]
    added = [masked_sum(member, optical) for member, optical in zip(members, opticals)]
    fronts = []
    for member, back in zip(members, backs):
        same = jnp.dot(back, member, preferred_element_type=jnp.float32)
        fronts.append(jnp.where(nearer, same, 0.0).astype(jnp.bfloat16))
    depths = [added[0]]
    for value in added[1:]:
        depths.append(depths[-1] + value)
    throughs = []
    for at, (front, back, optical) in enumerate(zip(fronts, backs, opticals)):
        before = masked_sum(front, optical)
        if at > 0:
            before = before + masked_sum(back, split(depths[at - 1]))
        throughs.append(jnp.exp(-before))
    color = None
    for start, member, through in zip(starts, members, throughs):
        both = jnp.concatenate([through, through], axis=1)
        shaded = split(sorted_ref[start : start + block, : 2 * lanes] * both)
        shaded = masked_sum(member, shaded)
        color = shaded if color is None else color + shaded
    tiles = (group_count, out_ref.shape[2], lanes)
    out_ref[:, 0] = color[:, :lanes].reshape(tiles)
    out_ref[:, 1] = color[:, lanes:].reshape(tiles)
    out_ref[:, 2] = (1.0 - jnp.exp(-depths[-1])).reshape(tiles)


def composite(places, arrays, picks, late, slots, slot_count, group_count):
    smem, vmem = pl.BlockSpec(memory_space=pltpu.SMEM), pl.BlockSpec(memory_space=pltpu.VMEM)
    hbm = pl.BlockSpec(memory_space=pltpu.HBM)
    held = (sum(array not in late for array, _ in picks),) + arrays[0].shape[-3:]
    specs = [vmem if at in late else hbm for at in range(len(arrays))]
    arrays = [
        array if at in late else pltpu.with_memory_space_constraint(array, pltpu.HBM)
        for at, array in enumerate(arrays)
    ]
    return pl.pallas_call(
        functools.partial(composite_kernel, picks, late),
        in_specs=[smem, vmem] + specs,
        out_specs=vmem,
        out_shape=jax.ShapeDtypeStruct(
            (group_count, 3, slot_count // group_count, LANES), jnp.float32
        ),
        scratch_shapes=[
            pltpu.VMEM((slots.shape[1], 3 * LANES), jnp.float32),
            pltpu.VMEM(held, jnp.float32),
            pltpu.SemaphoreType.DMA(held[:1]),
        ],
        compiler_params=pltpu.CompilerParams(vmem_limit_bytes=VMEM_BYTES),
    )(places, slots, *arrays)


def depth_slots(tile_list, tile_slot, brick_rank, after):
    swap_count, brick_count = brick_rank.shape
    numbers = jnp.arange(brick_count, dtype=jnp.int32)
    placed = brick_rank[:, None, :] == numbers[None, :, None]
    found = tile_list[..., None] == jnp.arange(tile_slot.shape[0], dtype=jnp.int32)
    slots = jnp.sum(jnp.where(found, tile_slot, 0), axis=-1)
    slots = jnp.einsum(
        "srb,sbf->srf",
        placed.astype(jnp.float32),
        slots.reshape(swap_count, brick_count, -1).astype(jnp.float32),
        precision=lax.Precision.HIGHEST,
    ).reshape(1, -1)
    vmem = pl.BlockSpec(memory_space=pltpu.VMEM)
    return pl.pallas_call(
        slots_kernel,
        in_specs=[vmem] + [pl.BlockSpec(memory_space=pl.ANY)] * len(after),
        out_specs=vmem,
        out_shape=jax.ShapeDtypeStruct(slots.shape, jnp.float32),
        compiler_params=pltpu.CompilerParams(vmem_limit_bytes=VMEM_BYTES // 4),
        cost_estimate=pl.CostEstimate(flops=30000000000, bytes_accessed=0, transcendentals=0),
    )(slots, *after)


def chunk_shards(samples, tile_list, tile_slot, brick_rank):
    group_count = lax.axis_size("grp")
    swap_count = lax.axis_size("swap")
    device = lax.axis_index("grp").astype(jnp.int32)
    slab = lax.axis_index("swap").astype(jnp.int32)
    per_device, pixels = samples.shape[2], samples.shape[4]
    slot_count = tile_slot.shape[0]
    owned = slot_count // group_count
    numbers = jnp.stack([device, slab])
    mine = samples[0, 0]
    near = group_count // 2
    chunk = (3, per_device, LANES)

    def send(array, offset, flip):
        pairs = [
            (g * swap_count + s, (g ^ offset) * swap_count + (s ^ flip))
            for g in range(group_count)
            for s in range(swap_count)
        ]
        return lax.ppermute(array, ("grp", "swap"), pairs)

    relayed, direct = list(range(near, group_count - 4)), list(range(group_count - 4, group_count))
    leaving = on_device(
        functools.partial(pair_kernel, relayed[:2], []), [(2,) + chunk] * 2, numbers, mine
    )
    leaving += on_device(
        functools.partial(pair_kernel, relayed[2:], direct),
        [(2,) + chunk] * len(relayed[2:]) + [chunk] * (2 * len(direct)),
        numbers,
        mine,
    )
    (near_chunks,) = on_device(
        functools.partial(near_kernel, near), [(near * swap_count,) + chunk], numbers, mine
    )
    arrays, picks, sources = [], [], []

    def keep(array, entries):
        for index, source in entries:
            picks.append((len(arrays), index))
            sources.append(source)
        arrays.append(array)

    passing = []
    for offset, array in zip(relayed, leaving):
        got = send(array, offset, 0)
        keep(got, [(0, (offset, 0))])
        passing.append(got)
    singles = [(offset, flip) for offset in direct for flip in range(2)]
    for partner, array in zip(singles, leaving[len(relayed) :]):
        keep(send(array, *partner), [(None, partner)])
    late = set(range(1, len(arrays) + 1))
    for first, last in ((0, 4),):
        group = jnp.stack([got[1] for got in passing[first:last]])
        keep(
            send(group, 0, 1),
            [(at, (offset, 1)) for at, offset in enumerate(relayed[first:last])],
        )
    late.add(len(arrays))
    slots = depth_slots(tile_list, tile_slot, brick_rank, arrays)
    members = near * swap_count
    near_chunks = lax.all_to_all(
        near_chunks,
        ("grp", "swap"),
        split_axis=0,
        concat_axis=0,
        tiled=True,
        axis_index_groups=[list(range(members)), list(range(members, 2 * members))],
    )
    picks = [(0, at) for at in range(members)] + [(array + 1, index) for array, index in picks]
    arrays = [near_chunks] + arrays
    offsets = jnp.array([offset for offset, _ in sources], jnp.int32)
    flips = jnp.array([flip for _, flip in sources], jnp.int32)
    source = jnp.bitwise_xor(slab, flips) * group_count + jnp.bitwise_xor(device, offsets)
    entries = jnp.arange(members, dtype=jnp.int32)
    near_source = entries % swap_count * group_count + device // near * near + entries // swap_count
    source = jnp.concatenate([near_source, source])
    ranks = brick_rank.reshape(swap_count * group_count, BRICKS)
    ranks = ranks + jnp.repeat(jnp.arange(swap_count), group_count)[:, None] * brick_rank.shape[1]
    ids = jnp.arange(swap_count * group_count, dtype=jnp.int32)
    places = jnp.sum(jnp.where((source[:, None] == ids)[..., None], ranks[None], 0), axis=1)
    places = places.reshape(-1) * (per_device // BRICKS)
    tiles = composite(places, arrays, picks, late, slots, slot_count, group_count)
    image = lax.all_to_all(tiles, "grp", split_axis=0, concat_axis=0, tiled=True)
    red, green, opacity = (
        jnp.transpose(image[:, channel], (1, 0, 2)).reshape(owned, pixels // swap_count)
        for channel in range(3)
    )
    return jnp.stack([red, green, opacity - red, opacity], axis=1)[None]


def shards(samples, tile_list, tile_slot, brick_rank):
    device_count = lax.axis_size("grp") * lax.axis_size("swap")
    fragment_count = tile_list.shape[1] * tile_list.shape[2]
    if samples.shape[4] == device_count * LANES and fragment_count <= 1024:
        return chunk_shards(samples, tile_list, tile_slot, brick_rank)
    return general_shards(samples, tile_list, tile_slot, brick_rank)


def solution(mesh):
    return jax.shard_map(
        shards,
        mesh=mesh,
        in_specs=(P("swap", "grp", None, None, None), P(), P(), P()),
        out_specs=P("grp", None, None, "swap"),
        check_vma=False,
    )
```

```python
import functools
import jax
import jax.numpy as jnp
from jax import lax
from jax.experimental import pallas as pl
from jax.experimental.pallas import tpu as pltpu
from jax.sharding import PartitionSpec as P

BRICKS = 8


EXTINCTION = 0.024


def from_partner(array, axis, apart):
    return lax.ppermute(array, axis, [(i, i ^ 1 << apart) for i in range(lax.axis_size(axis))])


def render(values_in):
    depth_count = values_in.shape[1]
    shape = (values_in.shape[0], values_in.shape[2])
    before = jnp.zeros(shape, jnp.float32)
    red_sum = jnp.zeros(shape, jnp.float32)
    green_sum = jnp.zeros(shape, jnp.float32)
    blue_sum = jnp.zeros(shape, jnp.float32)
    for level in range(depth_count):
        values = values_in[:, level].astype(jnp.float32)
        extinction = EXTINCTION * values
        weight = jnp.exp(-before) * (1.0 - jnp.exp(-extinction))
        ratio = values / (1.0 + values)
        red_sum = red_sum + weight * ratio
        green_sum = green_sum + weight * 4.0 * ratio * (1.0 - ratio)
        blue_sum = blue_sum + weight * (1.0 - ratio)
        before = before + extinction
    return jnp.stack([red_sum, green_sum, blue_sum, before], axis=1)


def over_pair(front_part, back_part):
    colors = front_part[:, :3] + jnp.exp(-front_part[:, 3:4]) * back_part[:, :3]
    return jnp.concatenate([colors, front_part[:, 3:4] + back_part[:, 3:4]], axis=1)


def slot_tables(tiles_in, tile_slot, owned, per_brick, ranks_in):
    group_count, per_device = tiles_in.shape
    slot_ids = tile_slot[tiles_in]
    owners = slot_ids // owned
    tile_rows = slot_ids % owned
    position = jnp.arange(per_device, dtype=jnp.int32)
    same_owner = (owners[:, :, None] == owners[:, None, :]) & (
        position[None, None, :] < position[None, :, None]
    )
    places = jnp.sum(same_owner.astype(jnp.int32), axis=2)
    depth_keys = jnp.repeat(ranks_in.reshape(group_count, BRICKS), per_brick, axis=1)
    return (owners, tile_rows, places, depth_keys)


def arrivals(owners, tile_rows, places, depth_keys, device, capacity):
    slot_ids = jnp.arange(capacity, dtype=jnp.int32)
    matched = (
        (owners[:, None, :] == device) & (places[:, None, :] == slot_ids[None, :, None])
    ).astype(jnp.int32)
    rows_in = jnp.sum(matched * tile_rows[:, None, :], axis=2).reshape(-1)
    keys_in = jnp.sum(matched * depth_keys[:, None, :], axis=2).reshape(-1)
    valid_in = (jnp.sum(matched, axis=2) > 0).reshape(-1)
    return (rows_in, keys_in, valid_in)


def outgoing(fragments, owners_mine, places_mine, group_count, capacity):
    per_device = fragments.shape[0]
    target = owners_mine * capacity + places_mine
    slot_ids = jnp.arange(group_count * capacity, dtype=jnp.int32)
    matched = (target[None, :] == slot_ids[:, None]).astype(jnp.int32)
    numbers = jnp.arange(per_device, dtype=jnp.int32) + 1
    source = jnp.sum(matched * numbers[None, :], axis=1) - 1
    source = jnp.where(source < 0, per_device, source)
    padded = jnp.concatenate(
        [fragments, jnp.zeros((1,) + fragments.shape[1:], jnp.float32)], axis=0
    )
    return jnp.take(padded, source, axis=0)


def combine(pieces, rows_in, keys_in, valid_in, owned):
    optical = pieces[:, 3]
    both_valid = valid_in[:, None] & valid_in[None, :]
    in_front = (
        (rows_in[:, None] == rows_in[None, :]) & both_valid & (keys_in[None, :] < keys_in[:, None])
    ).astype(jnp.float32)
    prefix = jnp.dot(
        in_front, optical, precision=lax.Precision.HIGHEST, preferred_element_type=jnp.float32
    )
    shaded = pieces[:, :3] * jnp.exp(-prefix)[:, None]
    to_rows = (
        (jnp.arange(owned, dtype=jnp.int32)[:, None] == rows_in[None, :]) & valid_in[None, :]
    ).astype(jnp.float32)
    colors = jnp.einsum("of,fcp->ocp", to_rows, shaded, precision=lax.Precision.HIGHEST)
    summed = jnp.dot(
        to_rows, optical, precision=lax.Precision.HIGHEST, preferred_element_type=jnp.float32
    )
    return jnp.concatenate([colors, summed[:, None]], axis=1)


def leaving_of(fragments, owners_slab, places_slab, device, group_count, capacity):
    owners_mine = lax.dynamic_index_in_dim(owners_slab, device, 0, keepdims=False)
    places_mine = lax.dynamic_index_in_dim(places_slab, device, 0, keepdims=False)
    return outgoing(fragments, owners_mine, places_mine, group_count, capacity)


def general_shards(samples, tile_list, tile_slot, brick_rank):
    group_count = lax.axis_size("grp")
    swap_count = lax.axis_size("swap")
    device = lax.axis_index("grp")
    slab = lax.axis_index("swap")
    per_device = tile_list.shape[2]
    per_brick = per_device // BRICKS
    owned = tile_slot.shape[0] // group_count
    capacity = 2 * per_device // group_count
    pixels = samples.shape[4]
    block = pixels // swap_count
    fragments = render(samples[0, 0])
    tiles_slab = lax.dynamic_index_in_dim(tile_list, slab, 0, keepdims=False)
    ranks_slab = lax.dynamic_index_in_dim(brick_rank, slab, 0, keepdims=False)
    owners_slab, rows_slab, places_slab, keys_slab = slot_tables(
        tiles_slab, tile_slot, owned, per_brick, ranks_slab
    )
    leaving = leaving_of(fragments, owners_slab, places_slab, device, group_count, capacity)
    rows_in, keys_in, valid_in = arrivals(
        owners_slab, rows_slab, places_slab, keys_slab, device, capacity
    )
    arrived = lax.all_to_all(
        leaving.reshape(group_count, capacity, 4, pixels),
        "grp",
        split_axis=0,
        concat_axis=0,
        tiled=True,
    )
    partial_value = combine(
        arrived.reshape(-1, 4, arrived.shape[3]), rows_in, keys_in, valid_in, owned
    )
    levels = swap_count.bit_length() - 1
    partial_value = partial_value.reshape((owned, 4) + (2,) * levels + (block,))
    for level in range(levels):
        lower = partial_value[..., 0, :]
        upper = partial_value[..., 1, :]
        my_bit = jnp.right_shift(slab, level) % 2
        kept = jnp.where(my_bit == 1, upper, lower)
        given = jnp.where(my_bit == 1, lower, upper)
        received = from_partner(given, "swap", level)
        front_part = jnp.where(my_bit == 0, kept, received)
        back_part = jnp.where(my_bit == 0, received, kept)
        partial_value = over_pair(front_part, back_part)
    final_image = jnp.concatenate(
        [partial_value[:, :3], 1.0 - jnp.exp(-partial_value[:, 3:4])], axis=1
    )
    return final_image[None]


LANES = 128
VMEM_BYTES = 20 * 1024 * 1024


def level_order(fragments, depth_count):
    rows = fragments * depth_count
    to = lax.broadcasted_iota(jnp.int32, (rows, rows), 0)
    source = lax.broadcasted_iota(jnp.int32, (rows, rows), 1)
    wanted = (to % fragments) * depth_count + to // fragments
    return jnp.where(source == wanted, 1.0, 0.0).astype(jnp.bfloat16)


def render_levels(levels):
    before = through = held = held_twice = None
    for level in range(levels.shape[0]):
        values = levels[level]
        extinction = EXTINCTION * values
        before = extinction if before is None else before + extinction
        after = jnp.exp(-before)
        weight = (1.0 - after) if through is None else (through - after)
        through = after
        absent = 1.0 / (1.0 + values)
        once = weight * absent
        twice = once * absent
        held = once if held is None else held + once
        held_twice = twice if held_twice is None else held_twice + twice
    return (1.0 - through) - held, 4.0 * (held - held_twice), before


def render_pair(device, slab, samples_ref, order, offset):
    fragments, depth_count, pixels = samples_ref.shape
    half = pixels // 2
    picked = []
    for flip in range(2):
        first = jnp.bitwise_xor(slab, flip) * half + jnp.bitwise_xor(device, offset) * LANES
        picked.append(samples_ref[:, :, pl.ds(pl.multiple_of(first, LANES), LANES)])
    levels = jnp.dot(
        order,
        jnp.concatenate(picked, axis=2).reshape(fragments * depth_count, 2 * LANES),
        preferred_element_type=jnp.float32,
    ).reshape(depth_count, fragments, 2 * LANES)
    channels = render_levels(levels)
    return [[value[:, at * LANES : (at + 1) * LANES] for value in channels] for at in range(2)]


def pair_kernel(offsets, singles, numbers_ref, samples_ref, *out_refs):
    order = level_order(*samples_ref.shape[:2])
    targets = [[ref.at[0], ref.at[1]] for ref in out_refs[: len(offsets)]]
    rest = out_refs[len(offsets) :]
    targets += [rest[at : at + 2] for at in range(0, len(rest), 2)]
    for target, offset in zip(targets, offsets + singles):
        pair = render_pair(numbers_ref[0], numbers_ref[1], samples_ref, order, offset)
        for flip in range(2):
            for channel in range(3):
                target[flip][channel] = pair[flip][channel]


def near_kernel(near, numbers_ref, samples_ref, *refs):
    out_ref = refs[-1]
    order = level_order(*samples_ref.shape[:2])
    device, slab = numbers_ref[0], numbers_ref[1]
    for offset in range(near):
        pair = render_pair(device, slab, samples_ref, order, offset)
        for flip in range(2):
            entry = lax.rem(jnp.bitwise_xor(device, offset), near) * 2 + jnp.bitwise_xor(slab, flip)
            for channel in range(3):
                out_ref[entry, channel] = pair[flip][channel]


def on_device(kernel, out_shapes, numbers, *arrays):
    vmem = pl.BlockSpec(memory_space=pltpu.VMEM)
    return pl.pallas_call(
        kernel,
        in_specs=[pl.BlockSpec(memory_space=pltpu.SMEM)] + [vmem] * len(arrays),
        out_specs=[vmem] * len(out_shapes),
        out_shape=[jax.ShapeDtypeStruct(shape, jnp.float32) for shape in out_shapes],
        compiler_params=pltpu.CompilerParams(vmem_limit_bytes=VMEM_BYTES),
    )(numbers, *arrays)


def split(values):
    high = values.astype(jnp.bfloat16)
    low = (values - high.astype(jnp.float32)).astype(jnp.bfloat16)
    return jnp.concatenate([high, low], axis=1)


def masked_sum(mask, parts):
    both = jnp.dot(mask, parts, preferred_element_type=jnp.float32)
    width = parts.shape[1] // 2
    return both[:, :width] + both[:, width:]


def slots_kernel(slots_ref, *refs):
    refs[-1][...] = jnp.round(slots_ref[...])


def composite_kernel(picks, late, places_ref, slots_ref, *refs):
    count = 1 + max(array for array, _ in picks)
    chunk_refs, (out_ref, sorted_ref, held_ref, sems) = refs[:count], refs[count:]
    chunks, copies = [], []
    for array, index in picks:
        chunk = chunk_refs[array] if index is None else chunk_refs[array].at[index]
        if array in late:
            chunks.append((chunk, None))
        else:
            slot = len(copies)
            copies.append(pltpu.make_async_copy(chunk, held_ref.at[slot], sems.at[slot]))
            copies[-1].start()
            chunks.append((held_ref.at[slot], copies[-1]))
    channels, per_device, lanes = held_ref.shape[1:]
    fragment_count = sorted_ref.shape[0]
    group_count = out_ref.shape[0]
    per_brick = per_device // BRICKS
    for at in sorted(range(len(picks)), key=lambda at: chunks[at][1] is not None):
        chunk, copy = chunks[at]
        if copy is not None:
            copy.wait()
        for brick in range(BRICKS):
            place = pl.multiple_of(places_ref[at * BRICKS + brick], per_brick)
            rows = slice(brick * per_brick, (brick + 1) * per_brick)
            for channel in range(channels):
                sorted_ref[
                    pl.ds(place, per_brick), channel * lanes : (channel + 1) * lanes
                ] = chunk[channel, rows, :]
    block = min(2 * LANES, fragment_count)
    starts = range(0, fragment_count, block)
    row = lax.broadcasted_iota(jnp.int32, (block, block), 0) // per_brick
    column = lax.broadcasted_iota(jnp.int32, (block, block), 1) // per_brick
    nearer = column < row
    slot_count = group_count * out_ref.shape[2]
    slot_id = lax.broadcasted_iota(jnp.int32, (slot_count, block), 0).astype(jnp.float32)
    members, backs = [], []
    for start in starts:
        found = jnp.where(slots_ref[:, start : start + block] == slot_id, 1.0, 0.0)
        members.append(found.astype(jnp.bfloat16))
        backs.append(found.T.astype(jnp.bfloat16))
    opticals = [split(sorted_ref[start : start + block, 2 * lanes :]) for start in starts]
    added = [masked_sum(member, optical) for member, optical in zip(members, opticals)]
    fronts = []
    for member, back in zip(members, backs):
        same = jnp.dot(back, member, preferred_element_type=jnp.float32)
        fronts.append(jnp.where(nearer, same, 0.0).astype(jnp.bfloat16))
    depths = [added[0]]
    for value in added[1:]:
        depths.append(depths[-1] + value)
    throughs = []
    for at, (front, back, optical) in enumerate(zip(fronts, backs, opticals)):
        before = masked_sum(front, optical)
        if at > 0:
            before = before + masked_sum(back, split(depths[at - 1]))
        throughs.append(jnp.exp(-before))
    color = None
    for start, member, through in zip(starts, members, throughs):
        both = jnp.concatenate([through, through], axis=1)
        shaded = split(sorted_ref[start : start + block, : 2 * lanes] * both)
        shaded = masked_sum(member, shaded)
        color = shaded if color is None else color + shaded
    tiles = (group_count, out_ref.shape[2], lanes)
    out_ref[:, 0] = color[:, :lanes].reshape(tiles)
    out_ref[:, 1] = color[:, lanes:].reshape(tiles)
    out_ref[:, 2] = (1.0 - jnp.exp(-depths[-1])).reshape(tiles)


def composite(places, arrays, picks, late, slots, slot_count, group_count):
    smem, vmem = pl.BlockSpec(memory_space=pltpu.SMEM), pl.BlockSpec(memory_space=pltpu.VMEM)
    hbm = pl.BlockSpec(memory_space=pltpu.HBM)
    held = (sum(array not in late for array, _ in picks),) + arrays[0].shape[-3:]
    specs = [vmem if at in late else hbm for at in range(len(arrays))]
    arrays = [
        array if at in late else pltpu.with_memory_space_constraint(array, pltpu.HBM)
        for at, array in enumerate(arrays)
    ]
    return pl.pallas_call(
        functools.partial(composite_kernel, picks, late),
        in_specs=[smem, vmem] + specs,
        out_specs=vmem,
        out_shape=jax.ShapeDtypeStruct(
            (group_count, 3, slot_count // group_count, LANES), jnp.float32
        ),
        scratch_shapes=[
            pltpu.VMEM((slots.shape[1], 3 * LANES), jnp.float32),
            pltpu.VMEM(held, jnp.float32),
            pltpu.SemaphoreType.DMA(held[:1]),
        ],
        compiler_params=pltpu.CompilerParams(vmem_limit_bytes=VMEM_BYTES),
    )(places, slots, *arrays)


def depth_slots(tile_list, tile_slot, brick_rank, after):
    swap_count, brick_count = brick_rank.shape
    numbers = jnp.arange(brick_count, dtype=jnp.int32)
    placed = brick_rank[:, None, :] == numbers[None, :, None]
    found = tile_list[..., None] == jnp.arange(tile_slot.shape[0], dtype=jnp.int32)
    slots = jnp.sum(jnp.where(found, tile_slot, 0), axis=-1)
    slots = jnp.einsum(
        "srb,sbf->srf",
        placed.astype(jnp.float32),
        slots.reshape(swap_count, brick_count, -1).astype(jnp.float32),
        precision=lax.Precision.HIGHEST,
    ).reshape(1, -1)
    vmem = pl.BlockSpec(memory_space=pltpu.VMEM)
    return pl.pallas_call(
        slots_kernel,
        in_specs=[vmem] + [pl.BlockSpec(memory_space=pl.ANY)] * len(after),
        out_specs=vmem,
        out_shape=jax.ShapeDtypeStruct(slots.shape, jnp.float32),
        compiler_params=pltpu.CompilerParams(vmem_limit_bytes=VMEM_BYTES),
        cost_estimate=pl.CostEstimate(flops=30000000000, bytes_accessed=0, transcendentals=0),
    )(slots, *after)


def chunk_shards(samples, tile_list, tile_slot, brick_rank):
    group_count = lax.axis_size("grp")
    swap_count = lax.axis_size("swap")
    device = lax.axis_index("grp").astype(jnp.int32)
    slab = lax.axis_index("swap").astype(jnp.int32)
    per_device, pixels = samples.shape[2], samples.shape[4]
    slot_count = tile_slot.shape[0]
    owned = slot_count // group_count
    numbers = jnp.stack([device, slab])
    mine = samples[0, 0]
    near = group_count // 2
    chunk = (3, per_device, LANES)

    def send(array, offset, flip):
        pairs = [
            (g * swap_count + s, (g ^ offset) * swap_count + (s ^ flip))
            for g in range(group_count)
            for s in range(swap_count)
        ]
        return lax.ppermute(array, ("grp", "swap"), pairs)

    relayed, direct = list(range(near, group_count - 4)), list(range(group_count - 4, group_count))
    leaving = on_device(
        functools.partial(pair_kernel, relayed[:2], []), [(2,) + chunk] * 2, numbers, mine
    )
    leaving += on_device(
        functools.partial(pair_kernel, relayed[2:], direct),
        [(2,) + chunk] * len(relayed[2:]) + [chunk] * (2 * len(direct)),
        numbers,
        mine,
    )
    (near_chunks,) = on_device(
        functools.partial(near_kernel, near), [(near * swap_count,) + chunk], numbers, mine
    )
    arrays, picks, sources = [], [], []

    def keep(array, entries):
        for index, source in entries:
            picks.append((len(arrays), index))
            sources.append(source)
        arrays.append(array)

    passing = []
    for offset, array in zip(relayed, leaving):
        got = send(array, offset, 0)
        keep(got, [(0, (offset, 0))])
        passing.append(got)
    singles = [(offset, flip) for offset in direct for flip in range(2)]
    for partner, array in zip(singles, leaving[len(relayed) :]):
        keep(send(array, *partner), [(None, partner)])
    late = set(range(len(relayed) + 1, len(arrays) + 1))
    for first, last in ((0, 4),):
        group = jnp.stack([got[1] for got in passing[first:last]])
        keep(
            send(group, 0, 1),
            [(at, (offset, 1)) for at, offset in enumerate(relayed[first:last])],
        )
    late.add(len(arrays))
    low = group_count // 4
    owner, row = tile_slot // owned, tile_slot % owned
    exchange_slot = (owner % low * 4 + owner // low) * owned + row
    slots = depth_slots(tile_list, exchange_slot, brick_rank, arrays)
    members = near * swap_count
    near_chunks = lax.all_to_all(
        near_chunks,
        ("grp", "swap"),
        split_axis=0,
        concat_axis=0,
        tiled=True,
        axis_index_groups=[list(range(members)), list(range(members, 2 * members))],
    )
    picks = [(0, at) for at in range(members)] + [(array + 1, index) for array, index in picks]
    arrays = [near_chunks] + arrays
    offsets = jnp.array([offset for offset, _ in sources], jnp.int32)
    flips = jnp.array([flip for _, flip in sources], jnp.int32)
    source = jnp.bitwise_xor(slab, flips) * group_count + jnp.bitwise_xor(device, offsets)
    entries = jnp.arange(members, dtype=jnp.int32)
    near_source = entries % swap_count * group_count + device // near * near + entries // swap_count
    source = jnp.concatenate([near_source, source])
    ranks = brick_rank.reshape(swap_count * group_count, BRICKS)
    ranks = ranks + jnp.repeat(jnp.arange(swap_count), group_count)[:, None] * brick_rank.shape[1]
    ids = jnp.arange(swap_count * group_count, dtype=jnp.int32)
    places = jnp.sum(jnp.where((source[:, None] == ids)[..., None], ranks[None], 0), axis=1)
    places = places.reshape(-1) * (per_device // BRICKS)
    tiles = composite(places, arrays, picks, late, slots, slot_count, group_count)
    image = lax.all_to_all(
        tiles,
        "grp",
        split_axis=0,
        concat_axis=0,
        tiled=True,
        axis_index_groups=[[z * low + rest for rest in range(low) for z in range(4)]],
    )
    image = jnp.swapaxes(image.reshape((low, 4) + image.shape[1:]), 0, 1).reshape(image.shape)
    red, green, opacity = (
        jnp.transpose(image[:, channel], (1, 0, 2)).reshape(owned, pixels // swap_count)
        for channel in range(3)
    )
    return jnp.stack([red, green, opacity - red, opacity], axis=1)[None]


def shards(samples, tile_list, tile_slot, brick_rank):
    device_count = lax.axis_size("grp") * lax.axis_size("swap")
    fragment_count = tile_list.shape[1] * tile_list.shape[2]
    if samples.shape[4] == device_count * LANES and fragment_count <= 1024:
        return chunk_shards(samples, tile_list, tile_slot, brick_rank)
    return general_shards(samples, tile_list, tile_slot, brick_rank)


def solution(mesh):
    return jax.shard_map(
        shards,
        mesh=mesh,
        in_specs=(P("swap", "grp", None, None, None), P(), P(), P()),
        out_specs=P("grp", None, None, "swap"),
        check_vma=False,
    )
```

```python
import functools
import jax
import jax.numpy as jnp
from jax import lax
from jax.experimental import pallas as pl
from jax.experimental.pallas import tpu as pltpu
from jax.sharding import PartitionSpec as P

BRICKS = 8


EXTINCTION = 0.024


def from_partner(array, axis, apart):
    return lax.ppermute(array, axis, [(i, i ^ 1 << apart) for i in range(lax.axis_size(axis))])


def render(values_in):
    depth_count = values_in.shape[1]
    shape = (values_in.shape[0], values_in.shape[2])
    before = jnp.zeros(shape, jnp.float32)
    red_sum = jnp.zeros(shape, jnp.float32)
    green_sum = jnp.zeros(shape, jnp.float32)
    blue_sum = jnp.zeros(shape, jnp.float32)
    for level in range(depth_count):
        values = values_in[:, level].astype(jnp.float32)
        extinction = EXTINCTION * values
        weight = jnp.exp(-before) * (1.0 - jnp.exp(-extinction))
        ratio = values / (1.0 + values)
        red_sum = red_sum + weight * ratio
        green_sum = green_sum + weight * 4.0 * ratio * (1.0 - ratio)
        blue_sum = blue_sum + weight * (1.0 - ratio)
        before = before + extinction
    return jnp.stack([red_sum, green_sum, blue_sum, before], axis=1)


def over_pair(front_part, back_part):
    colors = front_part[:, :3] + jnp.exp(-front_part[:, 3:4]) * back_part[:, :3]
    return jnp.concatenate([colors, front_part[:, 3:4] + back_part[:, 3:4]], axis=1)


def slot_tables(tiles_in, tile_slot, owned, per_brick, ranks_in):
    group_count, per_device = tiles_in.shape
    slot_ids = tile_slot[tiles_in]
    owners = slot_ids // owned
    tile_rows = slot_ids % owned
    position = jnp.arange(per_device, dtype=jnp.int32)
    same_owner = (owners[:, :, None] == owners[:, None, :]) & (
        position[None, None, :] < position[None, :, None]
    )
    places = jnp.sum(same_owner.astype(jnp.int32), axis=2)
    depth_keys = jnp.repeat(ranks_in.reshape(group_count, BRICKS), per_brick, axis=1)
    return (owners, tile_rows, places, depth_keys)


def arrivals(owners, tile_rows, places, depth_keys, device, capacity):
    slot_ids = jnp.arange(capacity, dtype=jnp.int32)
    matched = (
        (owners[:, None, :] == device) & (places[:, None, :] == slot_ids[None, :, None])
    ).astype(jnp.int32)
    rows_in = jnp.sum(matched * tile_rows[:, None, :], axis=2).reshape(-1)
    keys_in = jnp.sum(matched * depth_keys[:, None, :], axis=2).reshape(-1)
    valid_in = (jnp.sum(matched, axis=2) > 0).reshape(-1)
    return (rows_in, keys_in, valid_in)


def outgoing(fragments, owners_mine, places_mine, group_count, capacity):
    per_device = fragments.shape[0]
    target = owners_mine * capacity + places_mine
    slot_ids = jnp.arange(group_count * capacity, dtype=jnp.int32)
    matched = (target[None, :] == slot_ids[:, None]).astype(jnp.int32)
    numbers = jnp.arange(per_device, dtype=jnp.int32) + 1
    source = jnp.sum(matched * numbers[None, :], axis=1) - 1
    source = jnp.where(source < 0, per_device, source)
    padded = jnp.concatenate(
        [fragments, jnp.zeros((1,) + fragments.shape[1:], jnp.float32)], axis=0
    )
    return jnp.take(padded, source, axis=0)


def combine(pieces, rows_in, keys_in, valid_in, owned):
    optical = pieces[:, 3]
    both_valid = valid_in[:, None] & valid_in[None, :]
    in_front = (
        (rows_in[:, None] == rows_in[None, :]) & both_valid & (keys_in[None, :] < keys_in[:, None])
    ).astype(jnp.float32)
    prefix = jnp.dot(
        in_front, optical, precision=lax.Precision.HIGHEST, preferred_element_type=jnp.float32
    )
    shaded = pieces[:, :3] * jnp.exp(-prefix)[:, None]
    to_rows = (
        (jnp.arange(owned, dtype=jnp.int32)[:, None] == rows_in[None, :]) & valid_in[None, :]
    ).astype(jnp.float32)
    colors = jnp.einsum("of,fcp->ocp", to_rows, shaded, precision=lax.Precision.HIGHEST)
    summed = jnp.dot(
        to_rows, optical, precision=lax.Precision.HIGHEST, preferred_element_type=jnp.float32
    )
    return jnp.concatenate([colors, summed[:, None]], axis=1)


def leaving_of(fragments, owners_slab, places_slab, device, group_count, capacity):
    owners_mine = lax.dynamic_index_in_dim(owners_slab, device, 0, keepdims=False)
    places_mine = lax.dynamic_index_in_dim(places_slab, device, 0, keepdims=False)
    return outgoing(fragments, owners_mine, places_mine, group_count, capacity)


def general_shards(samples, tile_list, tile_slot, brick_rank):
    group_count = lax.axis_size("grp")
    swap_count = lax.axis_size("swap")
    device = lax.axis_index("grp")
    slab = lax.axis_index("swap")
    per_device = tile_list.shape[2]
    per_brick = per_device // BRICKS
    owned = tile_slot.shape[0] // group_count
    capacity = 2 * per_device // group_count
    pixels = samples.shape[4]
    block = pixels // swap_count
    fragments = render(samples[0, 0])
    tiles_slab = lax.dynamic_index_in_dim(tile_list, slab, 0, keepdims=False)
    ranks_slab = lax.dynamic_index_in_dim(brick_rank, slab, 0, keepdims=False)
    owners_slab, rows_slab, places_slab, keys_slab = slot_tables(
        tiles_slab, tile_slot, owned, per_brick, ranks_slab
    )
    leaving = leaving_of(fragments, owners_slab, places_slab, device, group_count, capacity)
    rows_in, keys_in, valid_in = arrivals(
        owners_slab, rows_slab, places_slab, keys_slab, device, capacity
    )
    arrived = lax.all_to_all(
        leaving.reshape(group_count, capacity, 4, pixels),
        "grp",
        split_axis=0,
        concat_axis=0,
        tiled=True,
    )
    partial_value = combine(
        arrived.reshape(-1, 4, arrived.shape[3]), rows_in, keys_in, valid_in, owned
    )
    levels = swap_count.bit_length() - 1
    partial_value = partial_value.reshape((owned, 4) + (2,) * levels + (block,))
    for level in range(levels):
        lower = partial_value[..., 0, :]
        upper = partial_value[..., 1, :]
        my_bit = jnp.right_shift(slab, level) % 2
        kept = jnp.where(my_bit == 1, upper, lower)
        given = jnp.where(my_bit == 1, lower, upper)
        received = from_partner(given, "swap", level)
        front_part = jnp.where(my_bit == 0, kept, received)
        back_part = jnp.where(my_bit == 0, received, kept)
        partial_value = over_pair(front_part, back_part)
    final_image = jnp.concatenate(
        [partial_value[:, :3], 1.0 - jnp.exp(-partial_value[:, 3:4])], axis=1
    )
    return final_image[None]


LANES = 128
VMEM_BYTES = 20 * 1024 * 1024


def level_order(fragments, depth_count):
    rows = fragments * depth_count
    to = lax.broadcasted_iota(jnp.int32, (rows, rows), 0)
    source = lax.broadcasted_iota(jnp.int32, (rows, rows), 1)
    wanted = (to % fragments) * depth_count + to // fragments
    return jnp.where(source == wanted, 1.0, 0.0).astype(jnp.bfloat16)


def render_levels(levels):
    before = through = held = held_twice = None
    for level in range(levels.shape[0]):
        values = levels[level]
        extinction = EXTINCTION * values
        before = extinction if before is None else before + extinction
        after = jnp.exp(-before)
        weight = (1.0 - after) if through is None else (through - after)
        through = after
        absent = 1.0 / (1.0 + values)
        once = weight * absent
        twice = once * absent
        held = once if held is None else held + once
        held_twice = twice if held_twice is None else held_twice + twice
    return (1.0 - through) - held, 4.0 * (held - held_twice), before


def render_pair(device, slab, samples_ref, order, offset):
    fragments, depth_count, pixels = samples_ref.shape
    half = pixels // 2
    picked = []
    for flip in range(2):
        first = jnp.bitwise_xor(slab, flip) * half + jnp.bitwise_xor(device, offset) * LANES
        picked.append(samples_ref[:, :, pl.ds(pl.multiple_of(first, LANES), LANES)])
    levels = jnp.dot(
        order,
        jnp.concatenate(picked, axis=2).reshape(fragments * depth_count, 2 * LANES),
        preferred_element_type=jnp.float32,
    ).reshape(depth_count, fragments, 2 * LANES)
    channels = render_levels(levels)
    return [[value[:, at * LANES : (at + 1) * LANES] for value in channels] for at in range(2)]


def pair_kernel(offsets, singles, numbers_ref, samples_ref, *out_refs):
    order = level_order(*samples_ref.shape[:2])
    targets = [[ref.at[0], ref.at[1]] for ref in out_refs[: len(offsets)]]
    rest = out_refs[len(offsets) :]
    targets += [rest[at : at + 2] for at in range(0, len(rest), 2)]
    for target, offset in zip(targets, offsets + singles):
        pair = render_pair(numbers_ref[0], numbers_ref[1], samples_ref, order, offset)
        for flip in range(2):
            for channel in range(3):
                target[flip][channel] = pair[flip][channel]


def near_kernel(near, numbers_ref, samples_ref, *refs):
    out_ref = refs[-1]
    order = level_order(*samples_ref.shape[:2])
    device, slab = numbers_ref[0], numbers_ref[1]
    for offset in range(near):
        pair = render_pair(device, slab, samples_ref, order, offset)
        for flip in range(2):
            entry = lax.rem(jnp.bitwise_xor(device, offset), near) * 2 + jnp.bitwise_xor(slab, flip)
            for channel in range(3):
                out_ref[entry, channel] = pair[flip][channel]


def on_device(kernel, out_shapes, numbers, *arrays):
    vmem = pl.BlockSpec(memory_space=pltpu.VMEM)
    return pl.pallas_call(
        kernel,
        in_specs=[pl.BlockSpec(memory_space=pltpu.SMEM)] + [vmem] * len(arrays),
        out_specs=[vmem] * len(out_shapes),
        out_shape=[jax.ShapeDtypeStruct(shape, jnp.float32) for shape in out_shapes],
        compiler_params=pltpu.CompilerParams(vmem_limit_bytes=VMEM_BYTES),
    )(numbers, *arrays)


def split(values):
    high = values.astype(jnp.bfloat16)
    low = (values - high.astype(jnp.float32)).astype(jnp.bfloat16)
    return jnp.concatenate([high, low], axis=1)


def masked_sum(mask, parts):
    both = jnp.dot(mask, parts, preferred_element_type=jnp.float32)
    width = parts.shape[1] // 2
    return both[:, :width] + both[:, width:]


def slots_kernel(slots_ref, *refs):
    refs[-1][...] = jnp.round(slots_ref[...])


def composite_kernel(picks, late, places_ref, slots_ref, *refs):
    count = 1 + max(array for array, _ in picks)
    chunk_refs, (out_ref, sorted_ref, held_ref, sems) = refs[:count], refs[count:]
    chunks, copies = [], []
    for array, index in picks:
        chunk = chunk_refs[array] if index is None else chunk_refs[array].at[index]
        if array in late:
            chunks.append((chunk, None))
        else:
            slot = len(copies)
            copies.append(pltpu.make_async_copy(chunk, held_ref.at[slot], sems.at[slot]))
            copies[-1].start()
            chunks.append((held_ref.at[slot], copies[-1]))
    channels, per_device, lanes = held_ref.shape[1:]
    fragment_count = sorted_ref.shape[0]
    group_count = out_ref.shape[0]
    per_brick = per_device // BRICKS
    for at in sorted(range(len(picks)), key=lambda at: chunks[at][1] is not None):
        chunk, copy = chunks[at]
        if copy is not None:
            copy.wait()
        for brick in range(BRICKS):
            place = pl.multiple_of(places_ref[at * BRICKS + brick], per_brick)
            rows = slice(brick * per_brick, (brick + 1) * per_brick)
            for channel in range(channels):
                sorted_ref[
                    pl.ds(place, per_brick), channel * lanes : (channel + 1) * lanes
                ] = chunk[channel, rows, :]
    block = min(2 * LANES, fragment_count)
    starts = range(0, fragment_count, block)
    row = lax.broadcasted_iota(jnp.int32, (block, block), 0) // per_brick
    column = lax.broadcasted_iota(jnp.int32, (block, block), 1) // per_brick
    nearer = column < row
    slot_count = group_count * out_ref.shape[2]
    slot_id = lax.broadcasted_iota(jnp.int32, (slot_count, block), 0).astype(jnp.float32)
    members, backs = [], []
    for start in starts:
        found = jnp.where(slots_ref[:, start : start + block] == slot_id, 1.0, 0.0)
        members.append(found.astype(jnp.bfloat16))
        backs.append(found.T.astype(jnp.bfloat16))
    opticals = [split(sorted_ref[start : start + block, 2 * lanes :]) for start in starts]
    added = [masked_sum(member, optical) for member, optical in zip(members, opticals)]
    fronts = []
    for member, back in zip(members, backs):
        same = jnp.dot(back, member, preferred_element_type=jnp.float32)
        fronts.append(jnp.where(nearer, same, 0.0).astype(jnp.bfloat16))
    depths = [added[0]]
    for value in added[1:]:
        depths.append(depths[-1] + value)
    throughs = []
    for at, (front, back, optical) in enumerate(zip(fronts, backs, opticals)):
        before = masked_sum(front, optical)
        if at > 0:
            before = before + masked_sum(back, split(depths[at - 1]))
        throughs.append(jnp.exp(-before))
    color = None
    for start, member, through in zip(starts, members, throughs):
        both = jnp.concatenate([through, through], axis=1)
        shaded = split(sorted_ref[start : start + block, : 2 * lanes] * both)
        shaded = masked_sum(member, shaded)
        color = shaded if color is None else color + shaded
    tiles = (group_count, out_ref.shape[2], lanes)
    out_ref[:, 0] = color[:, :lanes].reshape(tiles)
    out_ref[:, 1] = color[:, lanes:].reshape(tiles)
    out_ref[:, 2] = (1.0 - jnp.exp(-depths[-1])).reshape(tiles)


def composite(places, arrays, picks, late, slots, slot_count, group_count):
    smem, vmem = pl.BlockSpec(memory_space=pltpu.SMEM), pl.BlockSpec(memory_space=pltpu.VMEM)
    hbm = pl.BlockSpec(memory_space=pltpu.HBM)
    held = (sum(array not in late for array, _ in picks),) + arrays[0].shape[-3:]
    specs = [vmem if at in late else hbm for at in range(len(arrays))]
    arrays = [
        array if at in late else pltpu.with_memory_space_constraint(array, pltpu.HBM)
        for at, array in enumerate(arrays)
    ]
    return pl.pallas_call(
        functools.partial(composite_kernel, picks, late),
        in_specs=[smem, vmem] + specs,
        out_specs=vmem,
        out_shape=jax.ShapeDtypeStruct(
            (group_count, 3, slot_count // group_count, LANES), jnp.float32
        ),
        scratch_shapes=[
            pltpu.VMEM((slots.shape[1], 3 * LANES), jnp.float32),
            pltpu.VMEM(held, jnp.float32),
            pltpu.SemaphoreType.DMA(held[:1]),
        ],
        compiler_params=pltpu.CompilerParams(vmem_limit_bytes=VMEM_BYTES),
    )(places, slots, *arrays)


def depth_slots(tile_list, tile_slot, brick_rank, after):
    swap_count, brick_count = brick_rank.shape
    numbers = jnp.arange(brick_count, dtype=jnp.int32)
    placed = brick_rank[:, None, :] == numbers[None, :, None]
    found = tile_list[..., None] == jnp.arange(tile_slot.shape[0], dtype=jnp.int32)
    slots = jnp.sum(jnp.where(found, tile_slot, 0), axis=-1)
    slots = jnp.einsum(
        "srb,sbf->srf",
        placed.astype(jnp.float32),
        slots.reshape(swap_count, brick_count, -1).astype(jnp.float32),
        precision=lax.Precision.HIGHEST,
    ).reshape(1, -1)
    vmem = pl.BlockSpec(memory_space=pltpu.VMEM)
    return pl.pallas_call(
        slots_kernel,
        in_specs=[vmem] + [pl.BlockSpec(memory_space=pl.ANY)] * len(after),
        out_specs=vmem,
        out_shape=jax.ShapeDtypeStruct(slots.shape, jnp.float32),
        compiler_params=pltpu.CompilerParams(vmem_limit_bytes=VMEM_BYTES),
        cost_estimate=pl.CostEstimate(flops=30000000000, bytes_accessed=0, transcendentals=0),
    )(slots, *after)


def chunk_shards(samples, tile_list, tile_slot, brick_rank):
    group_count = lax.axis_size("grp")
    swap_count = lax.axis_size("swap")
    device = lax.axis_index("grp").astype(jnp.int32)
    slab = lax.axis_index("swap").astype(jnp.int32)
    per_device, pixels = samples.shape[2], samples.shape[4]
    slot_count = tile_slot.shape[0]
    owned = slot_count // group_count
    numbers = jnp.stack([device, slab])
    mine = samples[0, 0]
    near = group_count // 2
    chunk = (3, per_device, LANES)

    def send(array, offset, flip):
        pairs = [
            (g * swap_count + s, (g ^ offset) * swap_count + (s ^ flip))
            for g in range(group_count)
            for s in range(swap_count)
        ]
        return lax.ppermute(array, ("grp", "swap"), pairs)

    relayed, direct = list(range(near, group_count - 4)), list(range(group_count - 4, group_count))
    leaving = on_device(
        functools.partial(pair_kernel, relayed[:2], []), [(2,) + chunk] * 2, numbers, mine
    )
    leaving += on_device(
        functools.partial(pair_kernel, relayed[2:], direct),
        [(2,) + chunk] * len(relayed[2:]) + [chunk] * (2 * len(direct)),
        numbers,
        mine,
    )
    (near_chunks,) = on_device(
        functools.partial(near_kernel, near), [(near * swap_count,) + chunk], numbers, mine
    )
    arrays, picks, sources = [], [], []

    def keep(array, entries):
        for index, source in entries:
            picks.append((len(arrays), index))
            sources.append(source)
        arrays.append(array)

    passing = []
    for offset, array in zip(relayed, leaving):
        got = send(array, offset, 0)
        keep(got, [(0, (offset, 0))])
        passing.append(got)
    singles = [(offset, flip) for offset in direct for flip in range(2)]
    for partner, array in zip(singles, leaving[len(relayed) :]):
        keep(send(array, *partner), [(None, partner)])
    late = set(range(1, len(arrays) + 1))
    for first, last in ((0, 4),):
        group = jnp.stack([got[1] for got in passing[first:last]])
        keep(
            send(group, 0, 1),
            [(at, (offset, 1)) for at, offset in enumerate(relayed[first:last])],
        )
    late.add(len(arrays))
    low = group_count // 4
    owner, row = tile_slot // owned, tile_slot % owned
    exchange_slot = (owner % low * 4 + owner // low) * owned + row
    slots = depth_slots(tile_list, exchange_slot, brick_rank, arrays)
    members = near * swap_count
    near_chunks = lax.all_to_all(
        near_chunks,
        ("grp", "swap"),
        split_axis=0,
        concat_axis=0,
        tiled=True,
        axis_index_groups=[list(range(members)), list(range(members, 2 * members))],
    )
    picks = [(0, at) for at in range(members)] + [(array + 1, index) for array, index in picks]
    arrays = [near_chunks] + arrays
    offsets = jnp.array([offset for offset, _ in sources], jnp.int32)
    flips = jnp.array([flip for _, flip in sources], jnp.int32)
    source = jnp.bitwise_xor(slab, flips) * group_count + jnp.bitwise_xor(device, offsets)
    entries = jnp.arange(members, dtype=jnp.int32)
    near_source = entries % swap_count * group_count + device // near * near + entries // swap_count
    source = jnp.concatenate([near_source, source])
    ranks = brick_rank.reshape(swap_count * group_count, BRICKS)
    ranks = ranks + jnp.repeat(jnp.arange(swap_count), group_count)[:, None] * brick_rank.shape[1]
    ids = jnp.arange(swap_count * group_count, dtype=jnp.int32)
    places = jnp.sum(jnp.where((source[:, None] == ids)[..., None], ranks[None], 0), axis=1)
    places = places.reshape(-1) * (per_device // BRICKS)
    tiles = composite(places, arrays, picks, late, slots, slot_count, group_count)
    image = lax.all_to_all(
        tiles,
        "grp",
        split_axis=0,
        concat_axis=0,
        tiled=True,
        axis_index_groups=[[z * low + rest for rest in range(low) for z in range(4)]],
    )
    image = jnp.swapaxes(image.reshape((low, 4) + image.shape[1:]), 0, 1).reshape(image.shape)
    red, green, opacity = (
        jnp.transpose(image[:, channel], (1, 0, 2)).reshape(owned, pixels // swap_count)
        for channel in range(3)
    )
    return jnp.stack([red, green, opacity - red, opacity], axis=1)[None]


def shards(samples, tile_list, tile_slot, brick_rank):
    device_count = lax.axis_size("grp") * lax.axis_size("swap")
    fragment_count = tile_list.shape[1] * tile_list.shape[2]
    if samples.shape[4] == device_count * LANES and fragment_count <= 1024:
        return chunk_shards(samples, tile_list, tile_slot, brick_rank)
    return general_shards(samples, tile_list, tile_slot, brick_rank)


def solution(mesh):
    return jax.shard_map(
        shards,
        mesh=mesh,
        in_specs=(P("swap", "grp", None, None, None), P(), P(), P()),
        out_specs=P("grp", None, None, "swap"),
        check_vma=False,
    )
```
